32 devices in a mesh: vec: 4 (over y, x), gz: 8 (over z, core).
Axes of the slice: x: 2, y: 2, z: 4, core: 2. Of those that a mesh axis runs over, the one named last changes fastest.
Arguments:
- vectors: bfloat16 [1024, 3, 2, 4096], P('vec', None, None, 'gz'), may hold values from -6 to 6
- links: float32 [3, 3, 3, 2, 4096], P(None, None, None, None, 'gz'), may hold values from -4 to 4
- dirs: int32 [6], replicated, may hold values from 0 to 5, each once
- moms: int32 [2, 3], replicated, may hold values from -2 to 2
Outputs:
- elementals: float32 [6, 2, 2, 1024, 1024], P(None, None, None, ('vec', 'gz'))
The draws below stay inside these ranges and needn't reach their ends.
Inputs may be any that keep to these rules, and one draw needn't show every extreme that they name: `dirs`: each of the six directions appears exactly once.
All inputs are finite; a program needn't handle non-finite values.
Results may differ from the reference program's by a relative error of at most 0.0039.
Values may be sent and summed in bfloat16 or wider, within the bound.
No kernel may reach another device: no remote copies, remote signals or barrier semaphores. Data moves between devices by JAX's collectives and lax.ppermute only.
A program may use at most 192 MiB of HBM per device.

```python
import math
import jax
import jax.numpy as jnp
from jax import lax

NVEC = 1024
LX = 32
LY = 8
NP = 2
NZ = 16
NS = 4096


def plant(values, rng, least, largest):
    longest = values.shape.index(max(values.shape))
    spots = []
    for shift in (0, 1):
        where = [jax.random.randint(jax.random.fold_in(rng, axis), (), 0, length) for axis, length in enumerate(values.shape)]
        where[longest] = (where[longest] + shift) % values.shape[longest]
        spots.append(tuple(where))
    return values.at[spots[0]].set(least).at[spots[1]].set(largest)


def shard_levels(own_key, dims, cuts, least, largest):
    factor_of = 1.0
    for dim, shards_of in cuts:
        heights = jax.random.uniform(jax.random.fold_in(jax.random.fold_in(own_key, 6), dim), (shards_of,), jnp.float32, least / len(cuts), largest / len(cuts))
        factor_of = factor_of * jnp.repeat(jnp.exp(heights), dims[dim] // shards_of).reshape((-1,) + (1,) * (len(dims) - 1 - dim))
    return factor_of


def normal_values(own_key, extent, spread, bound, shards=(), kind=jnp.bfloat16):
    loudness = shard_levels(own_key, extent, shards, -0.22, 0.18) if shards else 1.0
    array = jax.random.normal(own_key, extent, jnp.float32) * spread * loudness
    return jnp.minimum(jnp.maximum(array, -bound), bound).astype(kind)


def setup_inputs(seed: int = 0) -> dict:
    arg_keys = jax.random.split(jax.random.key(seed), 5)
    vectors = normal_values(arg_keys[0], (NVEC, 3, 2, NS), 1.0, 6.0, ((0, 4), (3, 8)))
    links = normal_values(arg_keys[1], (3, 3, 3, 2, NS), 0.577, 4.0, ((4, 8),), jnp.float32)
    dirs = jax.random.permutation(arg_keys[2], 6).astype(jnp.int32)
    moms = plant(jax.random.randint(arg_keys[3], (NP, 3), -2, 3), jax.random.fold_in(arg_keys[3], 1), -2, 2).astype(jnp.int32)
    return dict(vectors=vectors, links=links, dirs=dirs, moms=moms)


def colour_apply(link_real, link_imag, vec_real, vec_imag):
    out_real = jnp.float32(0.0)
    out_imag = jnp.float32(0.0)
    for column in range(3):
        left_real = link_real[None, :, column]
        left_imag = link_imag[None, :, column]
        right_real = vec_real[:, None, column]
        right_imag = vec_imag[:, None, column]
        out_real = out_real + left_real * right_real - left_imag * right_imag
        out_imag = out_imag + left_real * right_imag + left_imag * right_real
    return (out_real, out_imag)

def reference(vectors, links, dirs, moms):
    count = vectors.shape[0]
    field = vectors.reshape(count, 3, 2, NZ, LY, LX)
    gauge = links.reshape(3, 3, 3, 2, NZ, LY, LX)
    z_index, y_index, x_index = jnp.meshgrid(jnp.arange(NZ, dtype=jnp.int32), jnp.arange(LY, dtype=jnp.int32), jnp.arange(LX, dtype=jnp.int32), indexing='ij')
    momenta = moms.astype(jnp.float32)
    theta = (momenta[:, 0, None, None, None] * x_index.astype(jnp.float32) / LX + momenta[:, 1, None, None, None] * y_index.astype(jnp.float32) / LY + momenta[:, 2, None, None, None] * z_index.astype(jnp.float32) / NZ) * (2.0 * math.pi)
    cosine = jnp.cos(theta)[:, None, None]
    sine = jnp.sin(theta)[:, None, None]
    field_f = field.astype(jnp.float32)
    real_part = field_f[:, :, 0][None]
    imag_part = field_f[:, :, 1][None]
    phased = jnp.stack((cosine * real_part - sine * imag_part, sine * real_part + cosine * imag_part), axis=3).astype(jnp.bfloat16)
    phased = lax.optimization_barrier(phased).astype(jnp.float32)
    raw = []
    for direction in range(6):
        axis_index = direction % 3
        roll_axis = -1 - axis_index
        link = gauge[axis_index]
        if direction < 3:
            moved = jnp.roll(field_f, -1, axis=roll_axis)
            link_real = link[:, :, 0]
            link_imag = link[:, :, 1]
        else:
            moved = jnp.roll(field_f, 1, axis=roll_axis)
            behind = jnp.roll(link, 1, axis=roll_axis)
            link_real = jnp.swapaxes(behind[:, :, 0], 0, 1)
            link_imag = -jnp.swapaxes(behind[:, :, 1], 0, 1)
        disp_real, disp_imag = colour_apply(link_real, link_imag, moved[:, :, 0], moved[:, :, 1])
        rounded_real = disp_real.astype(jnp.bfloat16)
        rounded_imag = disp_imag.astype(jnp.bfloat16)
        right = jnp.stack((jnp.stack((rounded_real, rounded_imag), axis=2), jnp.stack((rounded_imag, -rounded_real), axis=2)), axis=0)
        right = lax.optimization_barrier(right).astype(jnp.float32)
        raw.append(jnp.einsum('picrzyx,qjcrzyx->pqij', phased, right))
    stacked = jnp.stack(raw, axis=0)
    select = (dirs[:, None] == jnp.arange(6, dtype=jnp.int32)[None, :]).astype(jnp.float32)
    chosen = jnp.einsum('dk,kpqij->dpqij', select, stacked, precision=lax.Precision.HIGHEST)
    return chosen * (1.0 / math.sqrt(3.0 * NS))
```

```python
import functools
import math

import jax
import jax.numpy as jnp
from jax import lax
from jax.experimental import pallas as pl
from jax.experimental.pallas import tpu as pltpu
from jax.sharding import PartitionSpec as P

LX = 32
LY = 8
PLANE = LX * LY
LANES = 128
CORES = 2
VMEM_BYTES = 48 * 1024 * 1024


def shifted(chunks, axis, sign):
    lane = lax.broadcasted_iota(jnp.int32, chunks[0].shape, 1)
    if axis == 0:
        near = LANES - 1 if sign > 0 else 1
        far = LX - 1 if sign > 0 else LANES - (LX - 1)
        edge = lax.rem(lane, LX) == (LX - 1 if sign > 0 else 0)
        return [jnp.where(edge, pltpu.roll(c, far, 1), pltpu.roll(c, near, 1)) for c in chunks]
    turned = [pltpu.roll(c, LANES - LX if sign > 0 else LX, 1) for c in chunks]
    inside = lane < LANES - LX if sign > 0 else lane >= LX
    count = len(chunks)
    return [jnp.where(inside, turned[n], turned[(n + sign) % count]) for n in range(count)]


def apply_link(moved, link, adjoint):
    for row in range(3):
        real = imag = None
        for column in range(3):
            link_real, link_imag = link(column, row) if adjoint else link(row, column)
            vec_real, vec_imag = moved[2 * column], moved[2 * column + 1]
            if adjoint:
                terms = (link_real * vec_real + link_imag * vec_imag, link_real * vec_imag - link_imag * vec_real)
            else:
                terms = (link_real * vec_real - link_imag * vec_imag, link_real * vec_imag + link_imag * vec_real)
            real, imag = terms if real is None else (real + terms[0], imag + terms[1])
        yield row, real, imag


def store_left(out_ref, block, slab, axis, sign_at, first, moved, link, phase_ref, momenta, rows, sites):
    lanes = pl.ds(first, LANES)
    for row, real, imag in apply_link(moved, link, sign_at == 0):
        for p in range(momenta):
            at = (((slab * 3 + axis) * 2 + sign_at) * momenta + p) * 2
            cosine = phase_ref[pl.ds(at, 1), lanes]
            sine = phase_ref[pl.ds(at + 1, 1), lanes]
            down = pl.ds((sign_at * momenta + p) * rows, rows)
            column = (slab * 6 + row * 2) * sites + first
            out_ref[0, block, down, pl.ds(column, LANES)] = (cosine * real - sine * imag).astype(jnp.bfloat16)
            out_ref[0, block, down, pl.ds(column + sites, LANES)] = (sine * real + cosine * imag).astype(jnp.bfloat16)


def left_xy_kernel(momenta, rows, sites, place_ref, own_ref, other_ref, link_ref, other_link_ref, phase_ref, out_ref, table):
    chunks = PLANE // LANES
    for slab, (vec_ref, slab_link_ref) in enumerate(((own_ref, link_ref), (other_ref, other_link_ref))):
        for axis in range(2):
            for plane in range(sites // PLANE):
                starts = [plane * PLANE + n * LANES for n in range(chunks)]
                behind = shifted([slab_link_ref[axis, :, pl.ds(at, LANES)] for at in starts], axis, -1)
                for n in range(chunks):
                    table[:, pl.ds(n * LANES, LANES)] = behind[n]
                parts = [
                    [vec_ref[0, 0, :, pl.ds(c * sites + at, LANES)].astype(jnp.float32) for at in starts] for c in range(6)
                ]
                for sign_at, sign in enumerate((-1, 1)):
                    moved = [shifted(part, axis, sign) for part in parts]
                    for n, at in enumerate(starts):
                        if sign_at == 0:
                            def link(a, b, n=n):
                                lanes = pl.ds(n * LANES, LANES)
                                return table[pl.ds((a * 3 + b) * 2, 1), lanes], table[pl.ds((a * 3 + b) * 2 + 1, 1), lanes]
                        else:
                            def link(a, b, at=at):
                                lanes = pl.ds(at, LANES)
                                return (
                                    slab_link_ref[axis, pl.ds((a * 3 + b) * 2, 1), lanes],
                                    slab_link_ref[axis, pl.ds((a * 3 + b) * 2 + 1, 1), lanes],
                                )
                        store_left(
                            out_ref, axis, slab, axis, sign_at, at, [m[n] for m in moved], link, phase_ref, momenta, rows, sites
                        )


def left_z_kernel(
    momenta, rows, sites, place_ref, own_ref, other_ref, first_ref, second_ref, link_ref, other_link_ref, below_ref,
    phase_ref, kept_ref, out_ref, table,
):
    core = place_ref[1]
    low = core == 0
    top = sites - PLANE
    own = lambda c, at: own_ref[0, 0, :, pl.ds(c * sites + at, LANES)].astype(jnp.float32)
    other = lambda c, at: other_ref[0, 0, :, pl.ds(c * sites + at, LANES)].astype(jnp.float32)
    first = lambda c, at: first_ref[0, :, pl.ds(c * PLANE + at, LANES)].astype(jnp.float32)
    second = lambda c, at: second_ref[0, :, pl.ds(c * PLANE + at, LANES)].astype(jnp.float32)
    for slab, (mine, theirs, slab_link_ref, beside_link_ref) in enumerate(
        ((own, other, link_ref, other_link_ref), (other, own, other_link_ref, link_ref))
    ):
        below_is_halo = low if slab == 0 else jnp.logical_not(low)
        halo_below, halo_above = (second, second) if slab == 0 else (first, first)
        for at in range(0, PLANE, LANES):
            beside = beside_link_ref[2, :, pl.ds(top + at, LANES)]
            table[:, pl.ds(at, LANES)] = jnp.where(below_is_halo, below_ref[:, pl.ds(at, LANES)], beside)
        for at in range(0, sites, LANES):
            for sign_at, sign in enumerate((-1, 1)):
                source = at + sign * PLANE
                if 0 <= source < sites:
                    moved = [mine(c, source) for c in range(6)]
                elif source < 0:
                    moved = [
                        jnp.where(below_is_halo, halo_below(c, at), theirs(c, top + at)) for c in range(6)
                    ]
                else:
                    moved = [
                        jnp.where(below_is_halo, theirs(c, at - top), halo_above(c, at - top)) for c in range(6)
                    ]
                if sign_at == 0 and source < 0:
                    link_from = lambda row, at=at: table[pl.ds(row, 1), pl.ds(at, LANES)]
                else:
                    place = source if sign_at == 0 else at
                    link_from = lambda row, place=place: slab_link_ref[2, pl.ds(row, 1), pl.ds(place, LANES)]
                link = lambda a, b, link_from=link_from: (link_from((a * 3 + b) * 2), link_from((a * 3 + b) * 2 + 1))
                store_left(out_ref, 0, slab, 2, sign_at, at, moved, link, phase_ref, momenta, rows, sites)


def product_kernel(sites, left_ref, own_ref, other_ref, out_ref, right):
    width = own_ref.shape[0]

    @pl.when(pl.program_id(0) == 0)
    def _():
        for slab, ref in enumerate((own_ref, other_ref)):
            base = slab * 6 * sites
            right[pl.ds(0, width), pl.ds(base, 6 * sites)] = ref[...]
            for colour in range(3):
                real_at, imag_at = 2 * colour * sites, (2 * colour + 1) * sites
                right[pl.ds(width, width), pl.ds(base + real_at, sites)] = ref[:, pl.ds(imag_at, sites)]
                right[pl.ds(width, width), pl.ds(base + imag_at, sites)] = -ref[:, pl.ds(real_at, sites)]

    sums = lax.dot_general(left_ref[0], right[...], (((1,), (1,)), ((), ())), preferred_element_type=jnp.float32)
    out_ref[0, 0] = sums[:, :width].astype(out_ref.dtype)
    out_ref[0, 1] = sums[:, width:].astype(out_ref.dtype)


def finish_kernel(pieces, momenta, rows, scale, place_ref, *refs):
    out_ref = refs[-1]
    for q in range(2):
        total = refs[0][0, q].astype(jnp.float32)
        for ref in refs[1:pieces]:
            total = total + ref[0, q].astype(jnp.float32)
        total = total * scale
        for p in range(momenta):
            out_ref[0, p, q] = total[p * rows : (p + 1) * rows]


def on_device(vectors, links, dirs, moms):
    count, sites = vectors.shape[0], vectors.shape[-1]
    momenta = moms.shape[0]
    groups, slabs = lax.axis_size("vec"), lax.axis_size("gz")
    chips = slabs // CORES
    half = chips // 2
    rows = count // slabs
    depth = sites // PLANE
    group, slab = lax.axis_index("vec"), lax.axis_index("gz")
    core, chip = slab % CORES, slab // CORES
    place = jnp.stack((chip, core)).astype(jnp.int32)

    across = [(i, i ^ 1) for i in range(slabs)]
    flat = vectors.reshape(count, 6 * sites)
    other = lax.ppermute(flat, "gz", across)

    edge = lax.dynamic_slice_in_dim(vectors, jnp.where(core == 0, 0, sites - PLANE), PLANE, axis=3)
    edge = edge.reshape(chips, CORES, rows, 6 * PLANE)
    same = lax.dynamic_index_in_dim(edge, core, 1, keepdims=False)
    cross = lax.dynamic_index_in_dim(edge, 1 - core, 1, keepdims=False)
    step = lambda i: (i - CORES if i % CORES == 0 else i + CORES) % slabs
    first = lax.ppermute(same, "gz", [(i, step(i)) for i in range(slabs)])
    second = lax.ppermute(cross, "gz", [(i, step(i) ^ 1) for i in range(slabs)])

    link_rows = links.reshape(3, 18, sites)
    other_links = lax.ppermute(link_rows, "gz", across)
    top = link_rows[2, :, sites - PLANE :]
    below = jnp.where(
        core == 0,
        lax.ppermute(top, "gz", [(i, (i + 1) % slabs) for i in range(slabs)]),
        lax.ppermute(top, "gz", [(i, (i + 2) % slabs) for i in range(slabs)]),
    )

    sites_at = jnp.arange(sites, dtype=jnp.int32)
    coordinates = (sites_at % LX, sites_at // LX % LY, sites_at // PLANE)
    extents = (LX, LY, depth * slabs)
    integers = moms.astype(jnp.float32)
    phases = []
    for which in (slab, slab ^ 1):
        for axis in range(3):
            for sign in (-1, 1):
                angle = 0.0
                for mu in range(3):
                    along = coordinates[mu] + (which * depth if mu == 2 else 0) + (sign if mu == axis else 0)
                    angle = angle + integers[:, mu, None] * along.astype(jnp.float32) / extents[mu]
                phases.append(angle)
    angles = jnp.stack(phases, axis=0) * (2.0 * math.pi)
    phases = jnp.stack((jnp.cos(angles), jnp.sin(angles)), axis=2).reshape(-1, sites)

    left_rows = 2 * momenta * rows
    width = 12 * sites
    blocks = lambda flat: flat.reshape(chips, CORES, rows, 6 * sites)
    whole = lambda array: pl.BlockSpec(array.shape, lambda n, place: (0,) * array.ndim)

    def left_side(odd):
        mine = lambda n, place: (place[0] ^ (2 * n + odd), place[1], 0, 0)
        halo = lambda n, place: (place[0] ^ (2 * n + odd), 0, 0)
        vec_spec = pl.BlockSpec((1, 1, rows, 6 * sites), mine)
        halo_spec = pl.BlockSpec((1, rows, 6 * PLANE), halo)
        shape = jax.ShapeDtypeStruct((half, 3, left_rows, width), jnp.bfloat16)
        params = pltpu.CompilerParams(vmem_limit_bytes=VMEM_BYTES)
        work = half * left_rows * width
        left = pl.pallas_call(
            functools.partial(left_xy_kernel, momenta, rows, sites),
            grid_spec=pltpu.PrefetchScalarGridSpec(
                num_scalar_prefetch=1,
                grid=(half,),
                in_specs=[vec_spec, vec_spec, whole(link_rows), whole(other_links), whole(phases)],
                out_specs=pl.BlockSpec((1, 2, left_rows, width), lambda n, place: (n, 0, 0, 0)),
                scratch_shapes=[pltpu.VMEM((18, PLANE), jnp.float32)],
            ),
            out_shape=shape,
            compiler_params=params,
            cost_estimate=pl.CostEstimate(flops=100 * work, bytes_accessed=4 * work, transcendentals=0),
            name="left_xy",
        )(place, blocks(flat), blocks(other), link_rows, other_links, phases)
        return pl.pallas_call(
            functools.partial(left_z_kernel, momenta, rows, sites),
            grid_spec=pltpu.PrefetchScalarGridSpec(
                num_scalar_prefetch=1,
                grid=(half,),
                in_specs=[
                    vec_spec, vec_spec, halo_spec, halo_spec, whole(link_rows), whole(other_links), whole(below),
                    whole(phases), pl.BlockSpec(memory_space=pl.ANY),
                ],
                out_specs=pl.BlockSpec((1, 1, left_rows, width), lambda n, place: (n, 2, 0, 0)),
                scratch_shapes=[pltpu.VMEM((18, PLANE), jnp.float32)],
            ),
            out_shape=shape,
            input_output_aliases={9: 0},
            compiler_params=params,
            cost_estimate=pl.CostEstimate(flops=50 * work, bytes_accessed=2 * work, transcendentals=0),
            name="left_z",
        )(place, blocks(flat), blocks(other), first, second, link_rows, other_links, below, phases, left)

    def product(left, mine, theirs, kind):
        left = left.reshape(half, 3 * left_rows, width)
        flops = 2 * half * 3 * left_rows * width * 2 * count
        return pl.pallas_call(
            functools.partial(product_kernel, sites),
            grid=(half,),
            in_specs=[
                pl.BlockSpec((1, 3 * left_rows, width), lambda n: (n, 0, 0)),
                pl.BlockSpec(mine.shape, lambda n: (0, 0)),
                pl.BlockSpec(theirs.shape, lambda n: (0, 0)),
            ],
            out_specs=pl.BlockSpec((1, 2, 3 * left_rows, count), lambda n: (n, 0, 0, 0)),
            out_shape=jax.ShapeDtypeStruct((half, 2, 3 * left_rows, count), kind),
            scratch_shapes=[pltpu.VMEM((2 * count, width), jnp.bfloat16)],
            compiler_params=pltpu.CompilerParams(vmem_limit_bytes=VMEM_BYTES),
            cost_estimate=pl.CostEstimate(flops=flops, bytes_accessed=2 * left.size + 4 * mine.size, transcendentals=0),
            name="product",
        )(left, mine, theirs)

    scale = 1.0 / math.sqrt(3.0 * sites * slabs)
    spots = 2 * (dirs % 3) + dirs // 3
    out_shape = jax.ShapeDtypeStruct((6, momenta, 2, rows, groups * count), jnp.float32)

    def finish(pieces, turn, result):
        at = jnp.concatenate((spots, (group ^ turn)[None])).astype(jnp.int32)
        piece_spec = pl.BlockSpec((1, 2, momenta * rows, count), lambda d, at: (0, 0, at[d], 0))
        in_specs = [piece_spec] * len(pieces)
        operands = list(pieces)
        aliases = {}
        if result is not None:
            in_specs.append(pl.BlockSpec(memory_space=pl.ANY))
            operands.append(result)
            aliases = {len(operands): 0}
        return pl.pallas_call(
            functools.partial(finish_kernel, len(pieces), momenta, rows, scale),
            grid_spec=pltpu.PrefetchScalarGridSpec(
                num_scalar_prefetch=1,
                grid=(6,),
                in_specs=in_specs,
                out_specs=pl.BlockSpec((1, momenta, 2, rows, count), lambda d, at: (d, 0, 0, 0, at[6])),
            ),
            out_shape=out_shape,
            input_output_aliases=aliases,
            compiler_params=pltpu.CompilerParams(vmem_limit_bytes=VMEM_BYTES),
            cost_estimate=pl.CostEstimate(
                flops=8 * rows * count * 24, bytes_accessed=4 * 24 * rows * count * 3, transcendentals=0
            ),
            name="finish",
        )(at, *operands)

    sent = left_side(1)
    kept = left_side(0)
    result = None
    for turn in range(groups):
        if turn == 0:
            mine, theirs = flat, other
        else:
            mine = lax.ppermute(flat, "vec", [(i, i ^ turn) for i in range(groups)])
            theirs = lax.ppermute(mine, "gz", across)
        away = product(sent, mine, theirs, jnp.bfloat16)
        received = lax.ppermute(away, "gz", [(i, i ^ CORES) for i in range(slabs)])
        home = product(kept, mine, theirs, jnp.float32)
        pieces = [(home, 2), (received, 2)]
        bit = 2
        while bit < chips:
            terms = [piece[bit // stride :: 2 * bit // stride].astype(jnp.float32) for piece, stride in pieces]
            away = functools.reduce(jnp.add, terms).astype(jnp.bfloat16)
            received = lax.ppermute(away, "gz", [(i, i ^ (CORES * bit)) for i in range(slabs)])
            pieces.append((received, 2 * bit))
            bit *= 2
        result = finish([piece for piece, _ in pieces], turn, result)
    return result


def solution(mesh):
    placed = (P("vec", None, None, "gz"), P(None, None, None, None, "gz"), P(), P())
    return jax.shard_map(
        on_device,
        mesh=mesh,
        in_specs=placed,
        out_specs=P(None, None, None, ("vec", "gz"), None),
        check_vma=False,
    )
```

```python
import functools
import math

import jax
import jax.numpy as jnp
from jax import lax
from jax.experimental import pallas as pl
from jax.experimental.pallas import tpu as pltpu
from jax.sharding import PartitionSpec as P

LX = 32
LY = 8
PLANE = LX * LY
LANES = 128
CORES = 2
VMEM_BYTES = 48 * 1024 * 1024
COST_SCALE = 1.0


def cost(work):
    return pl.CostEstimate(flops=int(work * COST_SCALE), bytes_accessed=1024, transcendentals=0)


def shifted(chunks, axis, sign):
    lane = lax.broadcasted_iota(jnp.int32, chunks[0].shape, 1)
    if axis == 0:
        near = LANES - 1 if sign > 0 else 1
        far = LX - 1 if sign > 0 else LANES - (LX - 1)
        edge = lax.rem(lane, LX) == (LX - 1 if sign > 0 else 0)
        return [jnp.where(edge, pltpu.roll(c, far, 1), pltpu.roll(c, near, 1)) for c in chunks]
    turned = [pltpu.roll(c, LANES - LX if sign > 0 else LX, 1) for c in chunks]
    inside = lane < LANES - LX if sign > 0 else lane >= LX
    count = len(chunks)
    return [jnp.where(inside, turned[n], turned[(n + sign) % count]) for n in range(count)]


def apply_link(moved, link, adjoint):
    for row in range(3):
        real = imag = None
        for column in range(3):
            link_real, link_imag = link(column, row) if adjoint else link(row, column)
            vec_real, vec_imag = moved[2 * column], moved[2 * column + 1]
            if adjoint:
                terms = (link_real * vec_real + link_imag * vec_imag, link_real * vec_imag - link_imag * vec_real)
            else:
                terms = (link_real * vec_real - link_imag * vec_imag, link_real * vec_imag + link_imag * vec_real)
            real, imag = terms if real is None else (real + terms[0], imag + terms[1])
        yield row, real, imag


def store_left(out_ref, base, slab, axis, sign_at, first, moved, link, phase_ref, momenta, rows, sites):
    lanes = pl.ds(first, LANES)
    for row, real, imag in apply_link(moved, link, sign_at == 0):
        for p in range(momenta):
            at = ((slab * 3 + axis) * 2 + sign_at) * momenta + p
            cosine = phase_ref[0, pl.ds(at, 1), lanes]
            sine = phase_ref[1, pl.ds(at, 1), lanes]
            down = pl.ds(base + (sign_at * momenta + p) * rows, rows)
            column = row * 2 * sites + first
            out_ref[0, down, pl.ds(column, LANES)] = (cosine * real - sine * imag).astype(jnp.bfloat16)
            out_ref[0, down, pl.ds(column + sites, LANES)] = (sine * real + cosine * imag).astype(jnp.bfloat16)


def phase_kernel(momenta, sites, extents, place_ref, moms_ref, out_ref, angles):
    flat = lax.broadcasted_iota(jnp.int32, (1, sites), 1)
    depth = sites // PLANE
    turns = [[moms_ref[p, mu].astype(jnp.float32) / extents[mu] for mu in range(3)] for p in range(momenta)]
    at = 0
    for slab in range(2):
        core = place_ref[1] if slab == 0 else 1 - place_ref[1]
        planes = flat // PLANE + (place_ref[0] * CORES + core) * depth
        coordinates = [c.astype(jnp.float32) for c in (lax.rem(flat, LX), lax.rem(flat // LX, LY), planes)]
        base = [sum(turns[p][mu] * coordinates[mu] for mu in range(3)) for p in range(momenta)]
        for axis in range(3):
            for sign in (-1.0, 1.0):
                for p in range(momenta):
                    angles[pl.ds(at, 1), :] = (base[p] + sign * turns[p][axis]) * (2.0 * math.pi)
                    at += 1
    out_ref[0] = jnp.cos(angles[...])
    out_ref[1] = jnp.sin(angles[...])


def edge_kernel(sites, place_ref, same_ref, cross_ref, same_out, cross_out):
    for ref, out in ((same_ref, same_out), (cross_ref, cross_out)):
        for c in range(6):
            lowest = ref[:, pl.ds(c * sites, PLANE)]
            highest = ref[:, pl.ds((c + 1) * sites - PLANE, PLANE)]
            out[:, pl.ds(c * PLANE, PLANE)] = jnp.where(place_ref[1] == 0, lowest, highest)


def left_xy_kernel(momenta, rows, sites, slab, place_ref, vec_ref, link_ref, phase_ref, out_ref, table):
    chunks = PLANE // LANES
    for axis in range(2):
        for plane in range(sites // PLANE):
            starts = [plane * PLANE + n * LANES for n in range(chunks)]
            behind = shifted([link_ref[axis, :, pl.ds(at, LANES)] for at in starts], axis, -1)
            for n in range(chunks):
                table[:, pl.ds(n * LANES, LANES)] = behind[n]
            parts = [[vec_ref[:, pl.ds(c * sites + at, LANES)].astype(jnp.float32) for at in starts] for c in range(6)]
            for sign_at, sign in enumerate((-1, 1)):
                moved = [shifted(part, axis, sign) for part in parts]
                for n, at in enumerate(starts):
                    if sign_at == 0:
                        source = lambda row, n=n: table[pl.ds(row, 1), pl.ds(n * LANES, LANES)]
                    else:
                        source = lambda row, at=at: link_ref[axis, pl.ds(row, 1), pl.ds(at, LANES)]
                    link = lambda a, b, source=source: (source((a * 3 + b) * 2), source((a * 3 + b) * 2 + 1))
                    store_left(
                        out_ref, axis * 2 * momenta * rows, slab, axis, sign_at, at, [m[n] for m in moved], link,
                        phase_ref, momenta, rows, sites,
                    )


def left_z_kernel(
    momenta, rows, sites, place_ref, own_ref, other_ref, first_ref, second_ref, link_ref, other_link_ref, phase_ref,
    *refs,
):
    low = place_ref[1] == 0
    top = sites - PLANE
    read = lambda ref, c, at: ref[:, pl.ds(c + at, LANES)].astype(jnp.float32)
    for slab in range(2):
        mine, theirs = (own_ref, other_ref) if slab == 0 else (other_ref, own_ref)
        links = link_ref if slab == 0 else other_link_ref
        below_is_halo = low if slab == 0 else jnp.logical_not(low)
        halo = second_ref if slab == 0 else first_ref
        for at in range(0, sites, LANES):
            for sign_at, sign in enumerate((-1, 1)):
                source = at + sign * PLANE
                if 0 <= source < sites:
                    moved = [read(mine, c * sites, source) for c in range(6)]
                elif source < 0:
                    moved = [
                        jnp.where(below_is_halo, read(halo, c * PLANE, at), read(theirs, c * sites, top + at))
                        for c in range(6)
                    ]
                else:
                    moved = [
                        jnp.where(below_is_halo, read(theirs, c * sites, at - top), read(halo, c * PLANE, at - top))
                        for c in range(6)
                    ]
                kind = 3 if sign_at == 0 else 2
                value = lambda row, kind=kind, at=at: links[kind, pl.ds(row, 1), pl.ds(at, LANES)]
                link = lambda a, b, value=value: (value((a * 3 + b) * 2), value((a * 3 + b) * 2 + 1))
                store_left(refs[2 + slab], 0, slab, 2, sign_at, at, moved, link, phase_ref, momenta, rows, sites)


def product_kernel(sites, half, first_row, size, parts, received, *refs):
    mine, theirs = refs[:parts], refs[parts : 2 * parts]
    left = refs[2 * parts : 2 * parts + 2]
    got = refs[2 * parts + 2 : 2 * parts + 2 + received]
    *outs, right, rows, right_sems, left_sems = refs[2 * parts + 2 + received :]
    width = right.shape[0] // 2
    span = 6 * sites
    columns = [pl.ds(slab * span, span) for slab in range(2)]
    right_copies = [[], []]
    for slab, pieces in enumerate((mine, theirs)):
        start = 0
        for n, piece in enumerate(pieces):
            count = piece.shape[0]
            right_copies[slab].append(
                pltpu.make_async_copy(piece, right.at[pl.ds(start, count), columns[slab]], right_sems.at[slab, n])
            )
            start += count
    left_copies = [
        [
            pltpu.make_async_copy(
                left[slab].at[n, pl.ds(first_row, size)], rows.at[n, :, columns[slab]], left_sems.at[n, slab]
            )
            for slab in range(2)
        ]
        for n in range(half)
    ]
    for slab in range(2):
        for copy in right_copies[slab]:
            copy.start()
        left_copies[0][slab].start()
    for n in range(1, half):
        for slab in range(2):
            left_copies[n][slab].start()
    for n in range(half):
        sums = None
        for slab in range(2):
            if n == 0:
                for copy in right_copies[slab]:
                    copy.wait()
                for colour in range(3):
                    real_at = slab * span + 2 * colour * sites
                    imag_at = real_at + sites
                    right[pl.ds(width, width), pl.ds(real_at, sites)] = right[pl.ds(0, width), pl.ds(imag_at, sites)]
                    right[pl.ds(width, width), pl.ds(imag_at, sites)] = -right[pl.ds(0, width), pl.ds(real_at, sites)]
            left_copies[n][slab].wait()
            part = lax.dot_general(
                rows[n, :, columns[slab]], right[:, columns[slab]], (((1,), (1,)), ((), ())),
                preferred_element_type=jnp.float32,
            )
            sums = part if sums is None else sums + part
        out_ref = outs[n % len(outs)].at[n // len(outs)]
        for q in range(2):
            total = sums[:, q * width : (q + 1) * width]
            if not got:
                out_ref[q] = total.astype(out_ref.dtype)
            start = 0
            for ref in got:
                count = ref.shape[2]
                added = total[start : start + count] + ref[n, q].astype(jnp.float32)
                out_ref[q, pl.ds(start, count)] = added.astype(out_ref.dtype)
                start += count


def finish_kernel(pieces, momenta, rows, scale, place_ref, *refs):
    out_ref = refs[-1]
    size = momenta * rows
    for d in range(6):
        at = pl.ds(pl.multiple_of(place_ref[d] * size, size), size)
        for q in range(2):
            total = refs[0][0, q, at].astype(jnp.float32)
            for ref in refs[1:pieces]:
                total = total + ref[0, q, at].astype(jnp.float32)
            total = total * scale
            for p in range(momenta):
                out_ref[d, p, q] = total[p * rows : (p + 1) * rows]


def after(value, *earlier):
    return lax.optimization_barrier((value, *earlier))[0]


def on_device(vectors, links, dirs, moms):
    count, sites = vectors.shape[0], vectors.shape[-1]
    momenta = moms.shape[0]
    groups, slabs = lax.axis_size("vec"), lax.axis_size("gz")
    chips = slabs // CORES
    half = chips // 2
    rows = count // slabs
    depth = sites // PLANE
    span = 6 * sites
    group, slab = lax.axis_index("vec"), lax.axis_index("gz")
    core, chip = slab % CORES, slab // CORES
    place = jnp.stack((chip, core)).astype(jnp.int32)
    across = [(i, i ^ 1) for i in range(slabs)]
    params = pltpu.CompilerParams(vmem_limit_bytes=VMEM_BYTES)

    link_rows = links.reshape(3, 18, sites)
    top = link_rows[2, :, sites - PLANE :]
    other_links = lax.ppermute(link_rows, "gz", across)
    below = lax.ppermute(top, "gz", [(i, (i + 1) % slabs) for i in range(slabs)])
    two_below = lax.ppermute(top, "gz", [(i, (i + 2) % slabs) for i in range(slabs)])

    def with_shifted(link, lower):
        moved = jnp.concatenate((lower, link[2, :, : sites - PLANE]), axis=-1)
        return jnp.concatenate((link, moved[None]), axis=0)

    tables = with_shifted(link_rows, below)
    other_tables = with_shifted(other_links, jnp.where(core == 0, top, two_below))

    flat = after(vectors.reshape(count, span), other_links, below, two_below)
    other = lax.ppermute(flat, "gz", across)

    edge_shape = jax.ShapeDtypeStruct((chips * rows, 6 * PLANE), jnp.bfloat16)
    same, cross = pl.pallas_call(
        functools.partial(edge_kernel, sites),
        grid_spec=pltpu.PrefetchScalarGridSpec(
            num_scalar_prefetch=1,
            grid=(chips,),
            in_specs=[
                pl.BlockSpec((rows, span), lambda n, place: (n * CORES + place[1], 0)),
                pl.BlockSpec((rows, span), lambda n, place: (n * CORES + 1 - place[1], 0)),
            ],
            out_specs=[pl.BlockSpec((rows, 6 * PLANE), lambda n, place: (n, 0))] * 2,
        ),
        out_shape=[edge_shape] * 2,
        compiler_params=params,
        cost_estimate=cost(1e9),
        name="edges",
    )(place, flat, flat)
    step = lambda i: (i - CORES if i % CORES == 0 else i + CORES) % slabs
    first = lax.ppermute(same, "gz", [(i, step(i)) for i in range(slabs)])
    second = lax.ppermute(cross, "gz", [(i, step(i) ^ 1) for i in range(slabs)])

    phase_rows = 2 * 3 * 2 * momenta
    phases = pl.pallas_call(
        functools.partial(phase_kernel, momenta, sites, (LX, LY, depth * slabs)),
        in_specs=[pl.BlockSpec(memory_space=pltpu.SMEM)] * 2,
        out_shape=jax.ShapeDtypeStruct((2, phase_rows, sites), jnp.float32),
        scratch_shapes=[pltpu.VMEM((phase_rows, sites), jnp.float32)],
        compiler_params=params,
        cost_estimate=cost(1e9),
        name="phases",
    )(place, moms)

    left_rows = 6 * momenta * rows
    whole = lambda array: pl.BlockSpec(array.shape, lambda n, place: (0,) * array.ndim)
    left_shape = jax.ShapeDtypeStruct((half, left_rows, span), jnp.bfloat16)

    def left_specs(odd):
        mine = lambda n, place: ((place[0] ^ (2 * n + odd)) * CORES + place[1], 0)
        halo = lambda n, place: (place[0] ^ (2 * n + odd), 0)
        return pl.BlockSpec((rows, span), mine), pl.BlockSpec((rows, 6 * PLANE), halo)

    def left_xy(odd, which, vecs, table, place):
        return pl.pallas_call(
            functools.partial(left_xy_kernel, momenta, rows, sites, which),
            grid_spec=pltpu.PrefetchScalarGridSpec(
                num_scalar_prefetch=1,
                grid=(half,),
                in_specs=[left_specs(odd)[0], whole(table), whole(phases)],
                out_specs=pl.BlockSpec((1, 4 * momenta * rows, span), lambda n, place: (n, 0, 0)),
                scratch_shapes=[pltpu.VMEM((18, PLANE), jnp.float32)],
            ),
            out_shape=left_shape,
            compiler_params=params,
            cost_estimate=cost(4e9),
            name="left_xy",
        )(place, vecs, table, phases)

    def left_z(odd, sides):
        vec_spec, halo_spec = left_specs(odd)
        kept = pl.BlockSpec(memory_space=pl.ANY)
        return pl.pallas_call(
            functools.partial(left_z_kernel, momenta, rows, sites),
            grid_spec=pltpu.PrefetchScalarGridSpec(
                num_scalar_prefetch=1,
                grid=(half,),
                in_specs=[
                    vec_spec, vec_spec, halo_spec, halo_spec, whole(tables), whole(other_tables), whole(phases), kept, kept,
                ],
                out_specs=[pl.BlockSpec((1, 2 * momenta * rows, span), lambda n, place: (n, 2, 0))] * 2,
            ),
            out_shape=[left_shape] * 2,
            input_output_aliases={8: 0, 9: 1},
            compiler_params=params,
            cost_estimate=cost(5e9),
            name="left_z",
        )(place, flat, other, first, second, tables, other_tables, phases, *sides)

    def product(sides, mine, theirs, first_row=0, size=left_rows, received=()):
        width = sum(piece.shape[0] for piece in mine)
        kept = pl.BlockSpec(memory_space=pl.ANY)
        in_vmem = pl.BlockSpec(memory_space=pltpu.VMEM)
        shape = lambda n, kind: jax.ShapeDtypeStruct((n, 2, size, width), kind)
        if not received:
            shapes = [shape(half, jnp.bfloat16)]
        elif half == 1:
            shapes = [shape(1, jnp.float32)]
        else:
            shapes = [shape(half // 2, jnp.float32), shape(half // 2, jnp.bfloat16)]
        return pl.pallas_call(
            functools.partial(product_kernel, sites, half, first_row, size, len(mine), len(received)),
            in_specs=[kept] * (2 * len(mine) + 2) + [in_vmem] * len(received),
            out_specs=[in_vmem] * len(shapes),
            out_shape=shapes,
            scratch_shapes=[
                pltpu.VMEM((2 * width, 2 * span), jnp.bfloat16),
                pltpu.VMEM((half, size, 2 * span), jnp.bfloat16),
                pltpu.SemaphoreType.DMA((2, len(mine))),
                pltpu.SemaphoreType.DMA((half, 2)),
            ],
            compiler_params=params,
            cost_estimate=cost(7e9 * size / left_rows),
            name="product",
        )(*mine, *theirs, *sides, *received)

    scale = 1.0 / math.sqrt(3.0 * sites * slabs)
    spots = 2 * (dirs % 3) + dirs // 3
    out_shape = jax.ShapeDtypeStruct((6, momenta, 2, rows, groups * count), jnp.float32)

    def finish(pieces, places, result):
        at = jnp.concatenate((spots, jnp.stack(places))).astype(jnp.int32)
        in_specs = [pl.BlockSpec((1, 2, left_rows, LANES), lambda n, at: (0, 0, 0, n))] * len(pieces)
        operands = list(pieces)
        aliases = {}
        if result is not None:
            in_specs.append(pl.BlockSpec(memory_space=pl.ANY))
            operands.append(result)
            aliases = {len(operands): 0}
        return pl.pallas_call(
            functools.partial(finish_kernel, len(pieces), momenta, rows, scale),
            grid_spec=pltpu.PrefetchScalarGridSpec(
                num_scalar_prefetch=1,
                grid=(len(places),),
                in_specs=in_specs,
                out_specs=pl.BlockSpec((6, momenta, 2, rows, LANES), lambda n, at: (0, 0, 0, 0, at[6 + n])),
            ),
            out_shape=out_shape,
            input_output_aliases=aliases,
            compiler_params=params,
            cost_estimate=cost(3e9),
            name="finish",
        )(at, *operands)

    def to_chip(array, bit):
        return lax.ppermute(array, "gz", [(i, i ^ (CORES * bit)) for i in range(slabs)])

    def from_group(array, turn):
        return lax.ppermute(array, "vec", [(i, i ^ turn) for i in range(groups)])

    def to_core(arrays):
        return [lax.ppermute(array, "gz", across) for array in arrays]

    def reduce_more(kept, away=None):
        if away is None:
            return [kept]
        pieces, bit = [(kept, 4), (to_chip(away, 2), 4)], 4
        while bit < chips:
            terms = [piece[bit // stride :: 2 * bit // stride].astype(jnp.float32) for piece, stride in pieces]
            away = functools.reduce(jnp.add, terms).astype(jnp.bfloat16)
            pieces.append((to_chip(away, bit), 2 * bit))
            bit *= 2
        return [piece for piece, _ in pieces]

    part = count // 2
    split = groups > 2 and part % LANES == 0
    if split:
        blocks = [[(1, 0), (2, 0)], [(1, 1), (2, 1)]] + [[(turn, None)] for turn in range(3, groups)]
    else:
        blocks = [[(turn, None)] for turn in range(1, groups)]
    source = {None: flat, 0: flat[:part], 1: flat[part:]}
    wide = count // LANES

    def columns(block):
        places = []
        for turn, which in block:
            at = (group ^ turn) * wide
            places += [at + n for n in range(wide)] if which is None else [at + which * (wide // 2) + n for n in range(wide // 2)]
        return places

    def fetch(block, *earlier):
        return [from_group(after(source[which], *earlier) if earlier else source[which], turn) for turn, which in block]

    def own_columns(n):
        return columns([(0, None)] if n == 0 else blocks[n - 1])

    def pass_on(n, earlier):
        mine = [after(array, earlier) for array in arriving[n]]
        mine = [jnp.concatenate(mine, axis=0)] if len(mine) > 1 else mine
        if n < len(blocks):
            arriving[n + 1] = fetch(blocks[n], *mine)
        return mine, to_core(mine)

    arriving = {1: fetch(blocks[0])}
    right = {0: ([flat], [other])}
    flat_rows = 4 * momenta * rows
    odd = [left_xy(1, 0, flat, tables, place), left_xy(1, 1, other, other_tables, place)]
    (away,) = product(odd, *right[0], 0, flat_rows)
    received = {0: [to_chip(away, 1)]}
    odd = left_z(1, [after(odd[0], away), odd[1]])
    (away,) = product(odd, *right[0], flat_rows, left_rows - flat_rows)
    received[0].append(to_chip(away, 1))
    right[1] = pass_on(1, away)
    even = [left_xy(0, 0, flat, tables, after(place, away)), left_xy(0, 1, other, other_tables, after(place, away))]
    last = even[0]
    if len(blocks) > 1:
        right[2] = pass_on(2, last)
    even = left_z(0, [even[0], after(even[1], last)])
    last = even[0]
    sums = {}
    result = None
    for n in range(len(blocks) + 1):
        if n < len(blocks):
            (away,) = product([after(odd[0], last), odd[1]], *right[n + 1])
            received[n + 1] = [to_chip(away, 1)]
            last = away
            if n + 3 <= len(blocks):
                right[n + 3] = pass_on(n + 3, last)
        home = product([after(even[0], last), even[1]], *right[n], received=received[n])
        last = home[0]
        sums[n] = reduce_more(*home)
        if n > 0:
            ready = [after(sums[n - 1][0], last)] + sums[n - 1][1:]
            result = finish(ready, own_columns(n - 1), result)
            last = result
    return finish(sums[len(blocks)], own_columns(len(blocks)), result)


def solution(mesh):
    placed = (P("vec", None, None, "gz"), P(None, None, None, None, "gz"), P(), P())
    return jax.shard_map(
        on_device,
        mesh=mesh,
        in_specs=placed,
        out_specs=P(None, None, None, ("vec", "gz"), None),
        check_vma=False,
    )
```

```python
import functools
import math

import jax
import jax.numpy as jnp
from jax import lax
from jax.experimental import pallas as pl
from jax.experimental.pallas import tpu as pltpu
from jax.sharding import PartitionSpec as P

LX = 32
LY = 8
PLANE = LX * LY
LANES = 128
CORES = 2
VMEM_BYTES = 48 * 1024 * 1024
COST_SCALE = 1.0


def cost(work):
    return pl.CostEstimate(flops=int(work * COST_SCALE), bytes_accessed=1024, transcendentals=0)


def shifted(chunks, axis, sign):
    lane = lax.broadcasted_iota(jnp.int32, chunks[0].shape, 1)
    if axis == 0:
        near = LANES - 1 if sign > 0 else 1
        far = LX - 1 if sign > 0 else LANES - (LX - 1)
        edge = lax.rem(lane, LX) == (LX - 1 if sign > 0 else 0)
        return [jnp.where(edge, pltpu.roll(c, far, 1), pltpu.roll(c, near, 1)) for c in chunks]
    turned = [pltpu.roll(c, LANES - LX if sign > 0 else LX, 1) for c in chunks]
    inside = lane < LANES - LX if sign > 0 else lane >= LX
    count = len(chunks)
    return [jnp.where(inside, turned[n], turned[(n + sign) % count]) for n in range(count)]


def apply_link(moved, link, adjoint):
    for row in range(3):
        real = imag = None
        for column in range(3):
            link_real, link_imag = link(column, row) if adjoint else link(row, column)
            vec_real, vec_imag = moved[2 * column], moved[2 * column + 1]
            if adjoint:
                terms = (link_real * vec_real + link_imag * vec_imag, link_real * vec_imag - link_imag * vec_real)
            else:
                terms = (link_real * vec_real - link_imag * vec_imag, link_real * vec_imag + link_imag * vec_real)
            real, imag = terms if real is None else (real + terms[0], imag + terms[1])
        yield row, real, imag


def store_left(out_ref, base, slab, axis, sign_at, first, moved, link, phase_ref, momenta, rows, sites):
    lanes = pl.ds(first, LANES)
    for row, real, imag in apply_link(moved, link, sign_at == 0):
        for p in range(momenta):
            at = ((slab * 3 + axis) * 2 + sign_at) * momenta + p
            cosine = phase_ref[0, pl.ds(at, 1), lanes]
            sine = phase_ref[1, pl.ds(at, 1), lanes]
            down = pl.ds(base + (sign_at * momenta + p) * rows, rows)
            column = row * 2 * sites + first
            out_ref[0, down, pl.ds(column, LANES)] = (cosine * real - sine * imag).astype(jnp.bfloat16)
            out_ref[0, down, pl.ds(column + sites, LANES)] = (sine * real + cosine * imag).astype(jnp.bfloat16)


def phase_kernel(momenta, sites, extents, place_ref, moms_ref, out_ref, angles):
    flat = lax.broadcasted_iota(jnp.int32, (1, sites), 1)
    depth = sites // PLANE
    turns = [[moms_ref[p, mu].astype(jnp.float32) / extents[mu] for mu in range(3)] for p in range(momenta)]
    at = 0
    for slab in range(2):
        core = place_ref[1] if slab == 0 else 1 - place_ref[1]
        planes = flat // PLANE + (place_ref[0] * CORES + core) * depth
        coordinates = [c.astype(jnp.float32) for c in (lax.rem(flat, LX), lax.rem(flat // LX, LY), planes)]
        base = [sum(turns[p][mu] * coordinates[mu] for mu in range(3)) for p in range(momenta)]
        for axis in range(3):
            for sign in (-1.0, 1.0):
                for p in range(momenta):
                    angles[pl.ds(at, 1), :] = (base[p] + sign * turns[p][axis]) * (2.0 * math.pi)
                    at += 1
    out_ref[0] = jnp.cos(angles[...])
    out_ref[1] = jnp.sin(angles[...])


def edge_kernel(sites, place_ref, same_ref, cross_ref, same_out, cross_out):
    for ref, out in ((same_ref, same_out), (cross_ref, cross_out)):
        for c in range(6):
            lowest = ref[:, pl.ds(c * sites, PLANE)]
            highest = ref[:, pl.ds((c + 1) * sites - PLANE, PLANE)]
            out[:, pl.ds(c * PLANE, PLANE)] = jnp.where(place_ref[1] == 0, lowest, highest)


def left_xy_kernel(momenta, rows, sites, slab, place_ref, vec_ref, link_ref, phase_ref, out_ref, table):
    chunks = PLANE // LANES
    for axis in range(2):
        for plane in range(sites // PLANE):
            starts = [plane * PLANE + n * LANES for n in range(chunks)]
            behind = shifted([link_ref[axis, :, pl.ds(at, LANES)] for at in starts], axis, -1)
            for n in range(chunks):
                table[:, pl.ds(n * LANES, LANES)] = behind[n]
            parts = [[vec_ref[:, pl.ds(c * sites + at, LANES)].astype(jnp.float32) for at in starts] for c in range(6)]
            for sign_at, sign in enumerate((-1, 1)):
                moved = [shifted(part, axis, sign) for part in parts]
                for n, at in enumerate(starts):
                    if sign_at == 0:
                        source = lambda row, n=n: table[pl.ds(row, 1), pl.ds(n * LANES, LANES)]
                    else:
                        source = lambda row, at=at: link_ref[axis, pl.ds(row, 1), pl.ds(at, LANES)]
                    link = lambda a, b, source=source: (source((a * 3 + b) * 2), source((a * 3 + b) * 2 + 1))
                    store_left(
                        out_ref, axis * 2 * momenta * rows, slab, axis, sign_at, at, [m[n] for m in moved], link,
                        phase_ref, momenta, rows, sites,
                    )


def left_z_kernel(
    momenta, rows, sites, place_ref, own_ref, other_ref, first_ref, second_ref, link_ref, other_link_ref, phase_ref,
    *refs,
):
    low = place_ref[1] == 0
    top = sites - PLANE
    read = lambda ref, c, at: ref[:, pl.ds(c + at, LANES)].astype(jnp.float32)
    for slab in range(2):
        mine, theirs = (own_ref, other_ref) if slab == 0 else (other_ref, own_ref)
        links = link_ref if slab == 0 else other_link_ref
        below_is_halo = low if slab == 0 else jnp.logical_not(low)
        halo = second_ref if slab == 0 else first_ref
        for at in range(0, sites, LANES):
            for sign_at, sign in enumerate((-1, 1)):
                source = at + sign * PLANE
                if 0 <= source < sites:
                    moved = [read(mine, c * sites, source) for c in range(6)]
                elif source < 0:
                    moved = [
                        jnp.where(below_is_halo, read(halo, c * PLANE, at), read(theirs, c * sites, top + at))
                        for c in range(6)
                    ]
                else:
                    moved = [
                        jnp.where(below_is_halo, read(theirs, c * sites, at - top), read(halo, c * PLANE, at - top))
                        for c in range(6)
                    ]
                kind = 3 if sign_at == 0 else 2
                value = lambda row, kind=kind, at=at: links[kind, pl.ds(row, 1), pl.ds(at, LANES)]
                link = lambda a, b, value=value: (value((a * 3 + b) * 2), value((a * 3 + b) * 2 + 1))
                store_left(refs[2 + slab], 0, slab, 2, sign_at, at, moved, link, phase_ref, momenta, rows, sites)


def product_kernel(sites, half, first_row, size, parts, received, targets, *refs):
    mine, theirs = refs[:parts], refs[parts : 2 * parts]
    left = refs[2 * parts : 2 * parts + 2]
    got = refs[2 * parts + 2 : 2 * parts + 2 + received]
    *outs, right, rows, right_sems, left_sems = refs[2 * parts + 2 + received :]
    width = right.shape[0] // 2
    span = 6 * sites
    columns = [pl.ds(slab * span, span) for slab in range(2)]
    copies = [[], []]
    for slab, pieces in enumerate((mine, theirs)):
        start = 0
        for n, piece in enumerate(pieces):
            count = piece.shape[0]
            copies[slab].append(
                pltpu.make_async_copy(piece, right.at[pl.ds(start, count), columns[slab]], right_sems.at[slab, n])
            )
            start += count
        for n in range(half):
            copies[slab].append(
                pltpu.make_async_copy(
                    left[slab].at[n, pl.ds(first_row, size)], rows.at[pl.ds(n * size, size), columns[slab]],
                    left_sems.at[slab, n],
                )
            )
    for slab in range(2):
        for copy in copies[slab]:
            copy.start()
    sums = None
    for slab in range(2):
        for copy in copies[slab]:
            copy.wait()
        for colour in range(3):
            real_at = slab * span + 2 * colour * sites
            imag_at = real_at + sites
            right[pl.ds(width, width), pl.ds(real_at, sites)] = right[pl.ds(0, width), pl.ds(imag_at, sites)]
            right[pl.ds(width, width), pl.ds(imag_at, sites)] = -right[pl.ds(0, width), pl.ds(real_at, sites)]
        part = lax.dot_general(
            rows[:, columns[slab]], right[:, columns[slab]], (((1,), (1,)), ((), ())),
            preferred_element_type=jnp.float32,
        )
        sums = part if sums is None else sums + part
    for n, (which, place) in enumerate(targets):
        for q in range(2):
            total = sums[n * size : (n + 1) * size, q * width : (q + 1) * width]
            if not got:
                outs[which][place, q] = total.astype(outs[which].dtype)
            start = 0
            for ref in got:
                count = ref.shape[2]
                added = total[start : start + count] + ref[n, q].astype(jnp.float32)
                outs[which][place, q, pl.ds(start, count)] = added.astype(outs[which].dtype)
                start += count


def finish_kernel(pieces, momenta, rows, scale, place_ref, *refs):
    out_ref = refs[-1]
    size = momenta * rows
    for d in range(6):
        at = pl.ds(pl.multiple_of(place_ref[d] * size, size), size)
        for q in range(2):
            total = refs[0][0, q, at].astype(jnp.float32)
            for ref in refs[1:pieces]:
                total = total + ref[0, q, at].astype(jnp.float32)
            total = total * scale
            for p in range(momenta):
                out_ref[d, p, q] = total[p * rows : (p + 1) * rows]


def after(value, *earlier):
    return lax.optimization_barrier((value, *earlier))[0]


def order(last):
    steps = [("left", (1, 0)), ("left", (1, 1)), ("xy", 0), ("pass", 1), ("left_z", 1), ("z", 0)]
    steps += [("left", (0, 0)), ("left", (0, 1)), ("pass", 2), ("left_z", 0)]
    for n in range(max(last, 1)):
        if n + 1 < last:
            steps.append(("away", n + 1))
        elif n + 1 == last:
            steps += [("direct", 1), ("direct", 0)]
        steps.append(("home", n))
        if n > 0:
            steps.append(("finish", n - 1))
        if n + 1 < last:
            steps += [("pass", n + 3)] if n + 3 <= last else []
    return steps + [("finish", n) for n in range(max(last - 1, 0), last + 1)]


def on_device(vectors, links, dirs, moms):
    count, sites = vectors.shape[0], vectors.shape[-1]
    momenta = moms.shape[0]
    groups, slabs = lax.axis_size("vec"), lax.axis_size("gz")
    chips = slabs // CORES
    half = chips // 2
    rows = count // slabs
    depth = sites // PLANE
    span = 6 * sites
    group, slab = lax.axis_index("vec"), lax.axis_index("gz")
    core, chip = slab % CORES, slab // CORES
    place = jnp.stack((chip, core)).astype(jnp.int32)
    across = [(i, i ^ 1) for i in range(slabs)]
    params = pltpu.CompilerParams(vmem_limit_bytes=VMEM_BYTES)

    link_rows = links.reshape(3, 18, sites)
    top = link_rows[2, :, sites - PLANE :]
    other_links = lax.ppermute(link_rows, "gz", across)
    below = lax.ppermute(top, "gz", [(i, (i + 1) % slabs) for i in range(slabs)])
    two_below = lax.ppermute(top, "gz", [(i, (i + 2) % slabs) for i in range(slabs)])

    def with_shifted(link, lower):
        moved = jnp.concatenate((lower, link[2, :, : sites - PLANE]), axis=-1)
        return jnp.concatenate((link, moved[None]), axis=0)

    tables = with_shifted(link_rows, below)
    other_tables = with_shifted(other_links, jnp.where(core == 0, top, two_below))

    flat = after(vectors.reshape(count, span), other_links, below, two_below)
    other = lax.ppermute(flat, "gz", across)

    edge_shape = jax.ShapeDtypeStruct((chips * rows, 6 * PLANE), jnp.bfloat16)
    same, cross = pl.pallas_call(
        functools.partial(edge_kernel, sites),
        grid_spec=pltpu.PrefetchScalarGridSpec(
            num_scalar_prefetch=1,
            grid=(chips,),
            in_specs=[
                pl.BlockSpec((rows, span), lambda n, place: (n * CORES + place[1], 0)),
                pl.BlockSpec((rows, span), lambda n, place: (n * CORES + 1 - place[1], 0)),
            ],
            out_specs=[pl.BlockSpec((rows, 6 * PLANE), lambda n, place: (n, 0))] * 2,
        ),
        out_shape=[edge_shape] * 2,
        compiler_params=params,
        cost_estimate=cost(1e9),
        name="edges",
    )(place, flat, flat)
    step = lambda i: (i - CORES if i % CORES == 0 else i + CORES) % slabs
    first = lax.ppermute(same, "gz", [(i, step(i)) for i in range(slabs)])
    second = lax.ppermute(cross, "gz", [(i, step(i) ^ 1) for i in range(slabs)])

    phase_rows = 2 * 3 * 2 * momenta
    phases = pl.pallas_call(
        functools.partial(phase_kernel, momenta, sites, (LX, LY, depth * slabs)),
        in_specs=[pl.BlockSpec(memory_space=pltpu.SMEM)] * 2,
        out_shape=jax.ShapeDtypeStruct((2, phase_rows, sites), jnp.float32),
        scratch_shapes=[pltpu.VMEM((phase_rows, sites), jnp.float32)],
        compiler_params=params,
        cost_estimate=cost(1e9),
        name="phases",
    )(place, moms)

    left_rows = 6 * momenta * rows
    whole = lambda array: pl.BlockSpec(array.shape, lambda n, place: (0,) * array.ndim)
    left_shape = jax.ShapeDtypeStruct((half, left_rows, span), jnp.bfloat16)

    def left_specs(odd):
        mine = lambda n, place: ((place[0] ^ (2 * n + odd)) * CORES + place[1], 0)
        halo = lambda n, place: (place[0] ^ (2 * n + odd), 0)
        return pl.BlockSpec((rows, span), mine), pl.BlockSpec((rows, 6 * PLANE), halo)

    def left_xy(odd, which, vecs, table, place):
        return pl.pallas_call(
            functools.partial(left_xy_kernel, momenta, rows, sites, which),
            grid_spec=pltpu.PrefetchScalarGridSpec(
                num_scalar_prefetch=1,
                grid=(half,),
                in_specs=[left_specs(odd)[0], whole(table), whole(phases)],
                out_specs=pl.BlockSpec((1, 4 * momenta * rows, span), lambda n, place: (n, 0, 0)),
                scratch_shapes=[pltpu.VMEM((18, PLANE), jnp.float32)],
            ),
            out_shape=left_shape,
            compiler_params=params,
            cost_estimate=cost(4e9 if odd == 0 else 1e9),
            name="left_xy",
        )(place, vecs, table, phases)

    def left_z(odd, sides):
        vec_spec, halo_spec = left_specs(odd)
        kept = pl.BlockSpec(memory_space=pl.ANY)
        return pl.pallas_call(
            functools.partial(left_z_kernel, momenta, rows, sites),
            grid_spec=pltpu.PrefetchScalarGridSpec(
                num_scalar_prefetch=1,
                grid=(half,),
                in_specs=[
                    vec_spec, vec_spec, halo_spec, halo_spec, whole(tables), whole(other_tables), whole(phases), kept, kept,
                ],
                out_specs=[pl.BlockSpec((1, 2 * momenta * rows, span), lambda n, place: (n, 2, 0))] * 2,
            ),
            out_shape=[left_shape] * 2,
            input_output_aliases={8: 0, 9: 1},
            compiler_params=params,
            cost_estimate=cost(5e9),
            name="left_z",
        )(place, flat, other, first, second, tables, other_tables, phases, *sides)

    def product(sides, mine, theirs, targets, kinds, first_row=0, size=left_rows, received=()):
        width = sum(piece.shape[0] for piece in mine)
        kept = pl.BlockSpec(memory_space=pl.ANY)
        in_vmem = pl.BlockSpec(memory_space=pltpu.VMEM)
        chunks = [sum(which == n for which, _ in targets) for n in range(len(kinds))]
        return pl.pallas_call(
            functools.partial(product_kernel, sites, half, first_row, size, len(mine), len(received), targets),
            in_specs=[kept] * (2 * len(mine) + 2) + [in_vmem] * len(received),
            out_specs=[in_vmem] * len(kinds),
            out_shape=[jax.ShapeDtypeStruct((n, 2, size, width), kind) for n, kind in zip(chunks, kinds)],
            scratch_shapes=[
                pltpu.VMEM((2 * width, 2 * span), jnp.bfloat16),
                pltpu.VMEM((half * size, 2 * span), jnp.bfloat16),
                pltpu.SemaphoreType.DMA((2, len(mine))),
                pltpu.SemaphoreType.DMA((2, half)),
            ],
            compiler_params=params,
            cost_estimate=cost(7e9 * size / left_rows),
            name="product",
        )(*mine, *theirs, *sides, *received)

    def product_away(sides, right, *rows):
        (away,) = product(sides, *right, [(0, n) for n in range(half)], [jnp.bfloat16], *rows)
        return away, to_chip(away, 1)

    def product_home(sides, right, received):
        if half == 1:
            return product(sides, *right, [(0, 0)], [jnp.float32], received=received)
        targets = [(n % 2, n // 2) for n in range(half)]
        return product(sides, *right, targets, [jnp.float32, jnp.bfloat16], received=received)

    def product_direct(sides, right, odd):
        kinds = [jnp.float32 if n == 0 and not odd else jnp.bfloat16 for n in range(half)]
        outs = product(sides, *right, [(n, 0) for n in range(half)], kinds)
        return outs, [out if 2 * n + odd == 0 else to_chip(out, 2 * n + odd) for n, out in enumerate(outs)]

    scale = 1.0 / math.sqrt(3.0 * sites * slabs)
    spots = 2 * (dirs % 3) + dirs // 3
    out_shape = jax.ShapeDtypeStruct((6, momenta, 2, rows, groups * count), jnp.float32)

    def finish(pieces, places, result):
        at = jnp.concatenate((spots, jnp.stack(places))).astype(jnp.int32)
        in_specs = [pl.BlockSpec((1, 2, left_rows, LANES), lambda n, at: (0, 0, 0, n))] * len(pieces)
        operands = list(pieces)
        aliases = {}
        if result is not None:
            in_specs.append(pl.BlockSpec(memory_space=pl.ANY))
            operands.append(result)
            aliases = {len(operands): 0}
        return pl.pallas_call(
            functools.partial(finish_kernel, len(pieces), momenta, rows, scale),
            grid_spec=pltpu.PrefetchScalarGridSpec(
                num_scalar_prefetch=1,
                grid=(len(places),),
                in_specs=in_specs,
                out_specs=pl.BlockSpec((6, momenta, 2, rows, LANES), lambda n, at: (0, 0, 0, 0, at[6 + n])),
            ),
            out_shape=out_shape,
            input_output_aliases=aliases,
            compiler_params=params,
            cost_estimate=cost(3e9),
            name="finish",
        )(at, *operands)

    def to_chip(array, bit):
        return lax.ppermute(array, "gz", [(i, i ^ (CORES * bit)) for i in range(slabs)])

    def from_group(array, turn):
        return lax.ppermute(array, "vec", [(i, i ^ turn) for i in range(groups)])

    def to_core(arrays):
        return [lax.ppermute(array, "gz", across) for array in arrays]

    def reduce_more(kept, away=None):
        if away is None:
            return [kept]
        pieces, bit = [(kept, 4), (to_chip(away, 2), 4)], 4
        while bit < chips:
            terms = [piece[bit // stride :: 2 * bit // stride].astype(jnp.float32) for piece, stride in pieces]
            away = functools.reduce(jnp.add, terms).astype(jnp.bfloat16)
            pieces.append((to_chip(away, bit), 2 * bit))
            bit *= 2
        return [piece for piece, _ in pieces]

    part = count // 2
    split = groups > 2 and part % LANES == 0
    if split:
        blocks = [[(1, 0), (2, 0)], [(1, 1), (2, 1)]] + [[(turn, None)] for turn in range(3, groups)]
    else:
        blocks = [[(turn, None)] for turn in range(1, groups)]
    source = {None: flat, 0: flat[:part], 1: flat[part:]}
    wide = count // LANES

    def columns(block):
        places = []
        for turn, which in block:
            at = (group ^ turn) * wide
            places += [at + n for n in range(wide)] if which is None else [at + which * (wide // 2) + n for n in range(wide // 2)]
        return places

    def fetch(block, *earlier):
        return [from_group(after(source[which], *earlier) if earlier else source[which], turn) for turn, which in block]

    def own_columns(n):
        return columns([(0, None)] if n == 0 else blocks[n - 1])

    def pass_on(n, earlier):
        mine = [after(array, earlier) for array in arriving[n]]
        mine = [jnp.concatenate(mine, axis=0)] if len(mine) > 1 else mine
        if n < len(blocks):
            arriving[n + 1] = fetch(blocks[n], *mine)
        return mine, to_core(mine)

    def own_columns(n):
        return columns([(0, None)] if n == 0 else blocks[n - 1])

    def pass_on(n, earlier):
        if n not in arriving:
            return
        mine = [after(array, earlier) for array in arriving[n]]
        mine = [jnp.concatenate(mine, axis=0)] if len(mine) > 1 else mine
        if n < len(blocks):
            arriving[n + 1] = fetch(blocks[n], *mine)
        right[n] = (mine, to_core(mine))

    last = len(blocks)
    arriving = {1: fetch(blocks[0])} if blocks else {}
    right = {0: ([flat], [other])}
    flat_rows = 4 * momenta * rows
    sides = {1: [None, None], 0: [None, None]}
    received, sums = {0: []}, {}
    done, result = place, None

    def run(step, n):
        nonlocal done, result
        if step == "left":
            odd, which = n
            vecs, table = ((flat, tables), (other, other_tables))[which]
            sides[odd][which] = done = left_xy(odd, which, vecs, table, after(place, done))
        elif step == "left_z":
            sides[n] = left_z(n, [sides[n][0], after(sides[n][1], done)])
            done = sides[n][0]
        elif step == "pass":
            pass_on(n, done)
        elif step == "finish":
            result = done = finish([after(sums[n][0], done)] + sums[n][1:], own_columns(n), result)
        else:
            even = [after(sides[0][0], done), sides[0][1]]
            odd = [after(sides[1][0], done), sides[1][1]]
            if step == "xy":
                done, arrived = product_away(odd, right[n], 0, flat_rows)
                received[n].append(arrived)
            elif step == "z":
                done, arrived = product_away(odd, right[n], flat_rows, left_rows - flat_rows)
                received[n].append(arrived)
            elif step == "away":
                done, arrived = product_away(odd, right[n], 0, left_rows)
                received[n] = [arrived]
            elif step == "home":
                outs = product_home(even, right[n], received[n])
                sums[n], done = reduce_more(*outs), outs[0]
            elif step == "direct":
                outs, pieces = product_direct(odd if n else even, right[last], n)
                sums[last] = pieces + sums.get(last, []) if n == 0 else sums.get(last, []) + pieces
                done = outs[0]

    for step, n in order(last):
        run(step, n)
    return result


def solution(mesh):
    placed = (P("vec", None, None, "gz"), P(None, None, None, None, "gz"), P(), P())
    return jax.shard_map(
        on_device,
        mesh=mesh,
        in_specs=placed,
        out_specs=P(None, None, None, ("vec", "gz"), None),
        check_vma=False,
    )
```

```python
import functools
import math

import jax
import jax.numpy as jnp
from jax import lax
from jax.experimental import pallas as pl
from jax.experimental.pallas import tpu as pltpu
from jax.sharding import PartitionSpec as P

LX = 32
LY = 8
PLANE = LX * LY
LANES = 128
CORES = 2
VMEM_BYTES = 48 * 1024 * 1024
COST_SCALE = 1.0
ROWS = 384


def cost(work):
    return pl.CostEstimate(flops=int(work * COST_SCALE), bytes_accessed=1024, transcendentals=0)


def shifted(chunks, axis, sign):
    lane = lax.broadcasted_iota(jnp.int32, chunks[0].shape, 1)
    if axis == 0:
        near = LANES - 1 if sign > 0 else 1
        far = LX - 1 if sign > 0 else LANES - (LX - 1)
        edge = lax.rem(lane, LX) == (LX - 1 if sign > 0 else 0)
        return [jnp.where(edge, pltpu.roll(c, far, 1), pltpu.roll(c, near, 1)) for c in chunks]
    turned = [pltpu.roll(c, LANES - LX if sign > 0 else LX, 1) for c in chunks]
    inside = lane < LANES - LX if sign > 0 else lane >= LX
    count = len(chunks)
    return [jnp.where(inside, turned[n], turned[(n + sign) % count]) for n in range(count)]


def apply_link(moved, link, adjoint):
    for row in range(3):
        real = imag = None
        for column in range(3):
            link_real, link_imag = link(column, row) if adjoint else link(row, column)
            vec_real, vec_imag = moved[2 * column], moved[2 * column + 1]
            if adjoint:
                terms = (link_real * vec_real + link_imag * vec_imag, link_real * vec_imag - link_imag * vec_real)
            else:
                terms = (link_real * vec_real - link_imag * vec_imag, link_real * vec_imag + link_imag * vec_real)
            real, imag = terms if real is None else (real + terms[0], imag + terms[1])
        yield row, real, imag


def store_left(out_ref, base, slab, axis, sign_at, first, moved, link, phase_ref, momenta, rows, sites):
    lanes = pl.ds(first, LANES)
    for row, real, imag in apply_link(moved, link, sign_at == 0):
        for p in range(momenta):
            at = ((slab * 3 + axis) * 2 + sign_at) * momenta + p
            cosine = phase_ref[0, pl.ds(at, 1), lanes]
            sine = phase_ref[1, pl.ds(at, 1), lanes]
            down = pl.ds(base + (sign_at * momenta + p) * rows, rows)
            column = row * 2 * sites + first
            out_ref[0, down, pl.ds(column, LANES)] = (cosine * real - sine * imag).astype(jnp.bfloat16)
            out_ref[0, down, pl.ds(column + sites, LANES)] = (sine * real + cosine * imag).astype(jnp.bfloat16)


def phase_kernel(momenta, sites, extents, place_ref, moms_ref, out_ref, angles):
    flat = lax.broadcasted_iota(jnp.int32, (1, sites), 1)
    depth = sites // PLANE
    turns = [[moms_ref[p, mu].astype(jnp.float32) / extents[mu] for mu in range(3)] for p in range(momenta)]
    at = 0
    for slab in range(2):
        core = place_ref[1] if slab == 0 else 1 - place_ref[1]
        planes = flat // PLANE + (place_ref[0] * CORES + core) * depth
        coordinates = [c.astype(jnp.float32) for c in (lax.rem(flat, LX), lax.rem(flat // LX, LY), planes)]
        base = [sum(turns[p][mu] * coordinates[mu] for mu in range(3)) for p in range(momenta)]
        for axis in range(3):
            for sign in (-1.0, 1.0):
                for p in range(momenta):
                    angles[pl.ds(at, 1), :] = (base[p] + sign * turns[p][axis]) * (2.0 * math.pi)
                    at += 1
    out_ref[0] = jnp.cos(angles[...])
    out_ref[1] = jnp.sin(angles[...])


def edge_kernel(sites, place_ref, vec_ref, out_ref):
    for c in range(6):
        lowest = vec_ref[:, pl.ds(c * sites, PLANE)]
        highest = vec_ref[:, pl.ds((c + 1) * sites - PLANE, PLANE)]
        out_ref[:, pl.ds(c * PLANE, PLANE)] = jnp.where(place_ref[1] == 0, lowest, highest)


def left_xy_kernel(momenta, rows, sites, slab, place_ref, vec_ref, link_ref, phase_ref, out_ref, table):
    chunks = PLANE // LANES
    for axis in range(2):
        for plane in range(sites // PLANE):
            starts = [plane * PLANE + n * LANES for n in range(chunks)]
            behind = shifted([link_ref[axis, :, pl.ds(at, LANES)] for at in starts], axis, -1)
            for n in range(chunks):
                table[:, pl.ds(n * LANES, LANES)] = behind[n]
            parts = [[vec_ref[:, pl.ds(c * sites + at, LANES)].astype(jnp.float32) for at in starts] for c in range(6)]
            for sign_at, sign in enumerate((-1, 1)):
                moved = [shifted(part, axis, sign) for part in parts]
                for n, at in enumerate(starts):
                    if sign_at == 0:
                        source = lambda row, n=n: table[pl.ds(row, 1), pl.ds(n * LANES, LANES)]
                    else:
                        source = lambda row, at=at: link_ref[axis, pl.ds(row, 1), pl.ds(at, LANES)]
                    link = lambda a, b, source=source: (source((a * 3 + b) * 2), source((a * 3 + b) * 2 + 1))
                    store_left(
                        out_ref, axis * 2 * momenta * rows, slab, axis, sign_at, at, [m[n] for m in moved], link,
                        phase_ref, momenta, rows, sites,
                    )


def left_z_kernel(
    momenta, rows, sites, place_ref, own_ref, other_ref, first_ref, second_ref, link_ref, other_link_ref, phase_ref,
    *refs,
):
    low = place_ref[1] == 0
    top = sites - PLANE
    read = lambda ref, c, at: ref[:, pl.ds(c + at, LANES)].astype(jnp.float32)
    for slab in range(2):
        mine, theirs = (own_ref, other_ref) if slab == 0 else (other_ref, own_ref)
        links = link_ref if slab == 0 else other_link_ref
        below_is_halo = low if slab == 0 else jnp.logical_not(low)
        halo = second_ref if slab == 0 else first_ref
        for at in range(0, sites, LANES):
            for sign_at, sign in enumerate((-1, 1)):
                source = at + sign * PLANE
                if 0 <= source < sites:
                    moved = [read(mine, c * sites, source) for c in range(6)]
                elif source < 0:
                    moved = [
                        jnp.where(below_is_halo, read(halo, c * PLANE, at), read(theirs, c * sites, top + at))
                        for c in range(6)
                    ]
                else:
                    moved = [
                        jnp.where(below_is_halo, read(theirs, c * sites, at - top), read(halo, c * PLANE, at - top))
                        for c in range(6)
                    ]
                kind = 3 if sign_at == 0 else 2
                value = lambda row, kind=kind, at=at: links[kind, pl.ds(row, 1), pl.ds(at, LANES)]
                link = lambda a, b, value=value: (value((a * 3 + b) * 2), value((a * 3 + b) * 2 + 1))
                store_left(refs[2 + slab], 0, slab, 2, sign_at, at, moved, link, phase_ref, momenta, rows, sites)


def product_kernel(sites, half, first_row, size, parts, pairs, received, targets, *refs):
    mine, theirs = refs[:parts], refs[parts : 2 * parts]
    left = refs[2 * parts : 2 * parts + 2 * pairs]
    got = refs[2 * parts + 2 * pairs : 2 * parts + 2 * pairs + received]
    *outs, right, rows, right_sems, left_sems = refs[2 * parts + 2 * pairs + received :]
    width = right.shape[0] // 2
    span = 6 * sites
    chunks = half * pairs
    columns = [pl.ds(slab * span, span) for slab in range(2)]
    right_copies, left_copies = [[], []], [[], []]
    for slab, pieces in enumerate((mine, theirs)):
        start = 0
        for n, piece in enumerate(pieces):
            count = piece.shape[0]
            right_copies[slab].append(
                pltpu.make_async_copy(piece, right.at[pl.ds(start, count), columns[slab]], right_sems.at[slab, n])
            )
            start += count
        for n in range(chunks):
            left_copies[slab].append(
                pltpu.make_async_copy(
                    left[2 * (n // half) + slab].at[n % half, pl.ds(first_row, size)],
                    rows.at[pl.ds(n * size, size), columns[slab]], left_sems.at[slab, n],
                )
            )
    together = max(1, ROWS // size)
    groups = [range(n, min(n + together, chunks)) for n in range(0, chunks, together)]
    for group in groups:
        for slab in range(2):
            for copy in (right_copies[slab] if group is groups[0] else []) + [left_copies[slab][n] for n in group]:
                copy.start()
    for group in groups:
        sums = None
        here = pl.ds(group[0] * size, len(group) * size)
        for slab in range(2):
            if group is groups[0]:
                for copy in right_copies[slab]:
                    copy.wait()
                for colour in range(3):
                    real_at = slab * span + 2 * colour * sites
                    imag_at = real_at + sites
                    right[pl.ds(width, width), pl.ds(real_at, sites)] = right[pl.ds(0, width), pl.ds(imag_at, sites)]
                    right[pl.ds(width, width), pl.ds(imag_at, sites)] = -right[pl.ds(0, width), pl.ds(real_at, sites)]
            for n in group:
                left_copies[slab][n].wait()
            part = lax.dot_general(
                rows[here, columns[slab]], right[:, columns[slab]], (((1,), (1,)), ((), ())),
                preferred_element_type=jnp.float32,
            )
            sums = part if sums is None else sums + part
        for m, n in enumerate(group):
            which, place = targets[n]
            for q in range(2):
                total = sums[m * size : (m + 1) * size, q * width : (q + 1) * width]
                if not got:
                    outs[which][place, q] = total.astype(outs[which].dtype)
                start = 0
                for ref in got:
                    count = ref.shape[2]
                    added = total[start : start + count] + ref[n, q].astype(jnp.float32)
                    outs[which][place, q, pl.ds(start, count)] = added.astype(outs[which].dtype)
                    start += count


def finish_kernel(pieces, momenta, rows, scale, place_ref, *refs):
    out_ref = refs[-1]
    size = momenta * rows
    for d in range(6):
        at = pl.ds(pl.multiple_of(place_ref[d] * size, size), size)
        for q in range(2):
            total = refs[0][0, q, at].astype(jnp.float32)
            for ref in refs[1:pieces]:
                total = total + ref[0, q, at].astype(jnp.float32)
            total = total * scale
            for p in range(momenta):
                out_ref[d, p, q] = total[p * rows : (p + 1) * rows]


def after(value, *earlier):
    return lax.optimization_barrier((value, *earlier))[0]


def order(last):
    steps = [("left", (1, 0)), ("left", (1, 1)), ("xy", 0), ("halo", 0), ("pass", 1), ("left_z", 1), ("z", 0)]
    steps += [("left", (0, 0)), ("wait", 0), ("pass", 2), ("left", (0, 1)), ("left_z", 0)]
    if last > 1:
        steps.append(("away", 1))
    for n in range(max(last, 1)):
        if n + 1 == last:
            steps.append(("direct", last))
        if n + 2 < last:
            steps.append(("away", n + 2))
        steps.append(("home", n))
        if n + 3 <= last:
            steps.append(("pass", n + 3))
        if n > 0:
            steps.append(("finish", n - 1))
    return steps + [("finish", last)] + ([("finish", last - 1)] if last else [])


def on_device(vectors, links, dirs, moms):
    count, sites = vectors.shape[0], vectors.shape[-1]
    momenta = moms.shape[0]
    groups, slabs = lax.axis_size("vec"), lax.axis_size("gz")
    chips = slabs // CORES
    half = chips // 2
    rows = count // slabs
    depth = sites // PLANE
    span = 6 * sites
    group, slab = lax.axis_index("vec"), lax.axis_index("gz")
    core, chip = slab % CORES, slab // CORES
    place = jnp.stack((chip, core)).astype(jnp.int32)
    across = [(i, i ^ 1) for i in range(slabs)]
    params = pltpu.CompilerParams(vmem_limit_bytes=VMEM_BYTES)

    link_rows = links.reshape(3, 18, sites)
    top = link_rows[2, :, sites - PLANE :]
    other_links = lax.ppermute(link_rows, "gz", across)
    below = lax.ppermute(top, "gz", [(i, (i + 1) % slabs) for i in range(slabs)])
    two_below = lax.ppermute(top, "gz", [(i, (i + 2) % slabs) for i in range(slabs)])

    def with_shifted(link, lower):
        moved = jnp.concatenate((lower, link[2, :, : sites - PLANE]), axis=-1)
        return jnp.concatenate((link, moved[None]), axis=0)

    tables = with_shifted(link_rows, below)
    other_tables = with_shifted(other_links, jnp.where(core == 0, top, two_below))

    flat = after(vectors.reshape(count, span), other_links, below, two_below)
    other = lax.ppermute(flat, "gz", across)

    edge = pl.pallas_call(
        functools.partial(edge_kernel, sites),
        grid_spec=pltpu.PrefetchScalarGridSpec(
            num_scalar_prefetch=1,
            grid=(chips,),
            in_specs=[pl.BlockSpec((count // chips, span), lambda n, place: (n, 0))],
            out_specs=pl.BlockSpec((count // chips, 6 * PLANE), lambda n, place: (n, 0)),
        ),
        out_shape=jax.ShapeDtypeStruct((count, 6 * PLANE), jnp.bfloat16),
        compiler_params=params,
        cost_estimate=cost(1e9),
        name="edges",
    )(place, flat)
    step = lambda i: (i - CORES if i % CORES == 0 else i + CORES) % slabs
    halo = {0: lax.ppermute(edge, "gz", [(i, step(i)) for i in range(slabs)])}

    phase_rows = 2 * 3 * 2 * momenta
    phases = pl.pallas_call(
        functools.partial(phase_kernel, momenta, sites, (LX, LY, depth * slabs)),
        in_specs=[pl.BlockSpec(memory_space=pltpu.SMEM)] * 2,
        out_shape=jax.ShapeDtypeStruct((2, phase_rows, sites), jnp.float32),
        scratch_shapes=[pltpu.VMEM((phase_rows, sites), jnp.float32)],
        compiler_params=params,
        cost_estimate=cost(1e9),
        name="phases",
    )(place, moms)

    left_rows = 6 * momenta * rows
    whole = lambda array: pl.BlockSpec(array.shape, lambda n, place: (0,) * array.ndim)
    left_shape = jax.ShapeDtypeStruct((half, left_rows, span), jnp.bfloat16)

    def left_specs(odd):
        mine = lambda n, place: ((place[0] ^ (2 * n + odd)) * CORES + place[1], 0)
        return pl.BlockSpec((rows, span), mine), pl.BlockSpec((rows, 6 * PLANE), mine)

    def left_xy(odd, which, vecs, table, place):
        return pl.pallas_call(
            functools.partial(left_xy_kernel, momenta, rows, sites, which),
            grid_spec=pltpu.PrefetchScalarGridSpec(
                num_scalar_prefetch=1,
                grid=(half,),
                in_specs=[left_specs(odd)[0], whole(table), whole(phases)],
                out_specs=pl.BlockSpec((1, 4 * momenta * rows, span), lambda n, place: (n, 0, 0)),
                scratch_shapes=[pltpu.VMEM((18, PLANE), jnp.float32)],
            ),
            out_shape=left_shape,
            compiler_params=params,
            cost_estimate=cost(4e9 if odd == 0 else 0.5e9),
            name="left_xy",
        )(place, vecs, table, phases)

    def left_z(odd, sides):
        vec_spec, halo_spec = left_specs(odd)
        kept = pl.BlockSpec(memory_space=pl.ANY)
        return pl.pallas_call(
            functools.partial(left_z_kernel, momenta, rows, sites),
            grid_spec=pltpu.PrefetchScalarGridSpec(
                num_scalar_prefetch=1,
                grid=(half,),
                in_specs=[
                    vec_spec, vec_spec, halo_spec, halo_spec, whole(tables), whole(other_tables), whole(phases), kept, kept,
                ],
                out_specs=[pl.BlockSpec((1, 2 * momenta * rows, span), lambda n, place: (n, 2, 0))] * 2,
            ),
            out_shape=[left_shape] * 2,
            input_output_aliases={8: 0, 9: 1},
            compiler_params=params,
            cost_estimate=cost(5e9),
            name="left_z",
        )(place, flat, other, halo[0], halo[1], tables, other_tables, phases, *sides)

    def product(sides, mine, theirs, targets, kinds, first_row=0, size=left_rows, received=(), work=7e9):
        width = sum(piece.shape[0] for piece in mine)
        kept = pl.BlockSpec(memory_space=pl.ANY)
        in_vmem = pl.BlockSpec(memory_space=pltpu.VMEM)
        chunks = [sum(which == n for which, _ in targets) for n in range(len(kinds))]
        pairs = len(sides) // 2
        return pl.pallas_call(
            functools.partial(product_kernel, sites, half, first_row, size, len(mine), pairs, len(received), targets),
            in_specs=[kept] * (2 * len(mine) + len(sides)) + [in_vmem] * len(received),
            out_specs=[in_vmem] * len(kinds),
            out_shape=[jax.ShapeDtypeStruct((n, 2, size, width), kind) for n, kind in zip(chunks, kinds)],
            scratch_shapes=[
                pltpu.VMEM((2 * width, 2 * span), jnp.bfloat16),
                pltpu.VMEM((pairs * half * size, 2 * span), jnp.bfloat16),
                pltpu.SemaphoreType.DMA((2, len(mine))),
                pltpu.SemaphoreType.DMA((2, pairs * half)),
            ],
            compiler_params=params,
            cost_estimate=cost(work),
            name="product",
        )(*mine, *theirs, *sides, *received)

    def product_away(sides, right, first_row, size, work):
        (away,) = product(sides, *right, [(0, n) for n in range(half)], [jnp.bfloat16], first_row, size, work=work)
        return away, to_chip(away, 1)

    def product_home(sides, right, received, work):
        if half == 1:
            return product(sides, *right, [(0, 0)], [jnp.float32], received=received, work=work)
        targets = [(n % 2, n // 2) for n in range(half)]
        return product(sides, *right, targets, [jnp.float32, jnp.bfloat16], received=received, work=work)

    def product_direct(odd, even, right):
        kinds = [jnp.bfloat16] * half + [jnp.float32] + [jnp.bfloat16] * (half - 1)
        outs = product([*odd, *even], *right, [(n, 0) for n in range(chips)], kinds, work=1e9)
        far = [2 * n + 1 for n in range(half)] + [2 * n for n in range(half)]
        return outs[half], [out if s == 0 else to_chip(out, s) for s, out in zip(far, outs)]

    scale = 1.0 / math.sqrt(3.0 * sites * slabs)
    spots = 2 * (dirs % 3) + dirs // 3
    out_shape = jax.ShapeDtypeStruct((6, momenta, 2, rows, groups * count), jnp.float32)

    def finish(pieces, places, result):
        at = jnp.concatenate((spots, jnp.stack(places))).astype(jnp.int32)
        in_specs = [pl.BlockSpec((1, 2, left_rows, LANES), lambda n, at: (0, 0, 0, n))] * len(pieces)
        operands = list(pieces)
        aliases = {}
        if result is not None:
            in_specs.append(pl.BlockSpec(memory_space=pl.ANY))
            operands.append(result)
            aliases = {len(operands): 0}
        return pl.pallas_call(
            functools.partial(finish_kernel, len(pieces), momenta, rows, scale),
            grid_spec=pltpu.PrefetchScalarGridSpec(
                num_scalar_prefetch=1,
                grid=(len(places),),
                in_specs=in_specs,
                out_specs=pl.BlockSpec((6, momenta, 2, rows, LANES), lambda n, at: (0, 0, 0, 0, at[6 + n])),
            ),
            out_shape=out_shape,
            input_output_aliases=aliases,
            compiler_params=params,
            cost_estimate=cost(0.1e9),
            name="finish",
        )(at, *operands)

    def to_chip(array, bit):
        return lax.ppermute(array, "gz", [(i, i ^ (CORES * bit)) for i in range(slabs)])

    def from_group(array, turn):
        return lax.ppermute(array, "vec", [(i, i ^ turn) for i in range(groups)])

    def to_core(arrays):
        return [lax.ppermute(array, "gz", across) for array in arrays]

    def reduce_more(kept, away=None):
        if away is None:
            return [kept]
        pieces, bit = [(kept, 4), (to_chip(away, 2), 4)], 4
        while bit < chips:
            terms = [piece[bit // stride :: 2 * bit // stride].astype(jnp.float32) for piece, stride in pieces]
            away = functools.reduce(jnp.add, terms).astype(jnp.bfloat16)
            pieces.append((to_chip(away, bit), 2 * bit))
            bit *= 2
        return [piece for piece, _ in pieces]

    part = count // 2
    split = groups > 2 and part % LANES == 0
    if split:
        blocks = [[(1, 0), (2, 0)], [(1, 1), (2, 1)]] + [[(turn, None)] for turn in range(3, groups)]
    else:
        blocks = [[(turn, None)] for turn in range(1, groups)]
    source = {None: flat, 0: flat[:part], 1: flat[part:]}
    wide = count // LANES

    def columns(block):
        places = []
        for turn, which in block:
            at = (group ^ turn) * wide
            places += [at + n for n in range(wide)] if which is None else [at + which * (wide // 2) + n for n in range(wide // 2)]
        return places

    def fetch(block, *earlier):
        return [from_group(after(source[which], *earlier) if earlier else source[which], turn) for turn, which in block]

    def own_columns(n):
        return columns([(0, None)] if n == 0 else blocks[n - 1])

    def pass_on(n, earlier):
        mine = [after(array, earlier) for array in arriving[n]]
        mine = [jnp.concatenate(mine, axis=0)] if len(mine) > 1 else mine
        if n < len(blocks):
            arriving[n + 1] = fetch(blocks[n], *mine)
        return mine, to_core(mine)

    def own_columns(n):
        return columns([(0, None)] if n == 0 else blocks[n - 1])

    def pass_on(n, earlier):
        if n not in arriving:
            return
        mine = [after(array, earlier) for array in arriving[n]]
        mine = [jnp.concatenate(mine, axis=0)] if len(mine) > 1 else mine
        if n < len(blocks):
            arriving[n + 1] = fetch(blocks[n], *mine)
        right[n] = (mine, to_core(mine))

    last = len(blocks)
    arriving = {1: fetch(blocks[0])} if blocks else {}
    right = {0: ([flat], [other])}
    flat_rows = 4 * momenta * rows
    sides = {1: [None, None], 0: [None, None]}
    received, sums = {0: []}, {}
    done, result = place, None

    def run(step, n):
        nonlocal done, result
        if step == "left":
            odd, which = n
            vecs, table = ((flat, tables), (other, other_tables))[which]
            sides[odd][which] = done = left_xy(odd, which, vecs, table, after(place, done))
        elif step == "left_z":
            sides[n] = left_z(n, [sides[n][0], after(sides[n][1], done)])
            done = sides[n][0]
        elif step == "pass":
            pass_on(n, done)
        elif step == "halo":
            halo[1] = lax.ppermute(after(halo[0], done), "gz", across)
        elif step == "wait":
            done = after(done, received[n][0])
        elif step == "finish":
            result = done = finish([after(sums[n][0], done)] + sums[n][1:], own_columns(n), result)
        else:
            even = [after(sides[0][0], done), sides[0][1]]
            odd = [after(sides[1][0], done), sides[1][1]]
            if step == "xy":
                done, arrived = product_away(odd, right[n], 0, flat_rows, 1e9)
                received[n].append(arrived)
            elif step == "z":
                done, arrived = product_away(odd, right[n], flat_rows, left_rows - flat_rows, 2.5e9)
                received[n].append(arrived)
            elif step == "away":
                done, arrived = product_away(odd, right[n], 0, left_rows, 5e9)
                received[n] = [arrived]
            elif step == "home":
                outs = product_home(even, right[n], received[n], 2e9 if n == 0 else 10e9)
                sums[n], done = reduce_more(*outs), outs[0]
            elif step == "direct":
                done, sums[n] = product_direct(odd, even, right[n])

    for step, n in order(last):
        run(step, n)
    return result


def solution(mesh):
    placed = (P("vec", None, None, "gz"), P(None, None, None, None, "gz"), P(), P())
    return jax.shard_map(
        on_device,
        mesh=mesh,
        in_specs=placed,
        out_specs=P(None, None, None, ("vec", "gz"), None),
        check_vma=False,
    )
```

```python
import functools
import math

import jax
import jax.numpy as jnp
from jax import lax
from jax.experimental import pallas as pl
from jax.experimental.pallas import tpu as pltpu
from jax.sharding import PartitionSpec as P

LX = 32
LY = 8
PLANE = LX * LY
LANES = 128
CORES = 2
VMEM_BYTES = 48 * 1024 * 1024
COST_SCALE = 1.0
ROWS = 384


def cost(work):
    return pl.CostEstimate(flops=int(work * COST_SCALE), bytes_accessed=1024, transcendentals=0)


def shifted(chunks, axis, sign):
    lane = lax.broadcasted_iota(jnp.int32, chunks[0].shape, 1)
    if axis == 0:
        near = LANES - 1 if sign > 0 else 1
        far = LX - 1 if sign > 0 else LANES - (LX - 1)
        edge = lax.rem(lane, LX) == (LX - 1 if sign > 0 else 0)
        return [jnp.where(edge, pltpu.roll(c, far, 1), pltpu.roll(c, near, 1)) for c in chunks]
    turned = [pltpu.roll(c, LANES - LX if sign > 0 else LX, 1) for c in chunks]
    inside = lane < LANES - LX if sign > 0 else lane >= LX
    count = len(chunks)
    return [jnp.where(inside, turned[n], turned[(n + sign) % count]) for n in range(count)]


def apply_link(moved, link, adjoint):
    for row in range(3):
        real = imag = None
        for column in range(3):
            link_real, link_imag = link(column, row) if adjoint else link(row, column)
            vec_real, vec_imag = moved[2 * column], moved[2 * column + 1]
            if adjoint:
                terms = (link_real * vec_real + link_imag * vec_imag, link_real * vec_imag - link_imag * vec_real)
            else:
                terms = (link_real * vec_real - link_imag * vec_imag, link_real * vec_imag + link_imag * vec_real)
            real, imag = terms if real is None else (real + terms[0], imag + terms[1])
        yield row, real, imag


def store_left(out_ref, base, slab, axis, sign_at, first, moved, link, phase_ref, momenta, rows, sites):
    lanes = pl.ds(first, LANES)
    for row, real, imag in apply_link(moved, link, sign_at == 0):
        for p in range(momenta):
            at = ((slab * 3 + axis) * 2 + sign_at) * momenta + p
            cosine = phase_ref[0, pl.ds(at, 1), lanes]
            sine = phase_ref[1, pl.ds(at, 1), lanes]
            down = pl.ds(base + (sign_at * momenta + p) * rows, rows)
            column = row * 2 * sites + first
            out_ref[0, down, pl.ds(column, LANES)] = (cosine * real - sine * imag).astype(jnp.bfloat16)
            out_ref[0, down, pl.ds(column + sites, LANES)] = (sine * real + cosine * imag).astype(jnp.bfloat16)


def phase_kernel(momenta, sites, extents, place_ref, moms_ref, out_ref, angles):
    flat = lax.broadcasted_iota(jnp.int32, (1, sites), 1)
    depth = sites // PLANE
    turns = [[moms_ref[p, mu].astype(jnp.float32) / extents[mu] for mu in range(3)] for p in range(momenta)]
    at = 0
    for slab in range(2):
        core = place_ref[1] if slab == 0 else 1 - place_ref[1]
        planes = flat // PLANE + (place_ref[0] * CORES + core) * depth
        coordinates = [c.astype(jnp.float32) for c in (lax.rem(flat, LX), lax.rem(flat // LX, LY), planes)]
        base = [sum(turns[p][mu] * coordinates[mu] for mu in range(3)) for p in range(momenta)]
        for axis in range(3):
            for sign in (-1.0, 1.0):
                for p in range(momenta):
                    angles[pl.ds(at, 1), :] = (base[p] + sign * turns[p][axis]) * (2.0 * math.pi)
                    at += 1
    out_ref[0] = jnp.cos(angles[...])
    out_ref[1] = jnp.sin(angles[...])


def edge_kernel(sites, place_ref, vec_ref, out_ref):
    for c in range(6):
        lowest = vec_ref[:, pl.ds(c * sites, PLANE)]
        highest = vec_ref[:, pl.ds((c + 1) * sites - PLANE, PLANE)]
        out_ref[:, pl.ds(c * PLANE, PLANE)] = jnp.where(place_ref[1] == 0, lowest, highest)


def left_xy_kernel(momenta, rows, sites, slab, place_ref, vec_ref, link_ref, phase_ref, out_ref, table):
    chunks = PLANE // LANES
    for axis in range(2):
        for plane in range(sites // PLANE):
            starts = [plane * PLANE + n * LANES for n in range(chunks)]
            behind = shifted([link_ref[axis, :, pl.ds(at, LANES)] for at in starts], axis, -1)
            for n in range(chunks):
                table[:, pl.ds(n * LANES, LANES)] = behind[n]
            parts = [[vec_ref[:, pl.ds(c * sites + at, LANES)].astype(jnp.float32) for at in starts] for c in range(6)]
            for sign_at, sign in enumerate((-1, 1)):
                moved = [shifted(part, axis, sign) for part in parts]
                for n, at in enumerate(starts):
                    if sign_at == 0:
                        source = lambda row, n=n: table[pl.ds(row, 1), pl.ds(n * LANES, LANES)]
                    else:
                        source = lambda row, at=at: link_ref[axis, pl.ds(row, 1), pl.ds(at, LANES)]
                    link = lambda a, b, source=source: (source((a * 3 + b) * 2), source((a * 3 + b) * 2 + 1))
                    store_left(
                        out_ref, axis * 2 * momenta * rows, slab, axis, sign_at, at, [m[n] for m in moved], link,
                        phase_ref, momenta, rows, sites,
                    )


def left_z_kernel(
    momenta, rows, sites, place_ref, own_ref, other_ref, first_ref, second_ref, link_ref, other_link_ref, phase_ref,
    *refs,
):
    low = place_ref[1] == 0
    top = sites - PLANE
    read = lambda ref, c, at: ref[:, pl.ds(c + at, LANES)].astype(jnp.float32)
    for slab in range(2):
        mine, theirs = (own_ref, other_ref) if slab == 0 else (other_ref, own_ref)
        links = link_ref if slab == 0 else other_link_ref
        below_is_halo = low if slab == 0 else jnp.logical_not(low)
        halo = second_ref if slab == 0 else first_ref
        for at in range(0, sites, LANES):
            for sign_at, sign in enumerate((-1, 1)):
                source = at + sign * PLANE
                if 0 <= source < sites:
                    moved = [read(mine, c * sites, source) for c in range(6)]
                elif source < 0:
                    moved = [
                        jnp.where(below_is_halo, read(halo, c * PLANE, at), read(theirs, c * sites, top + at))
                        for c in range(6)
                    ]
                else:
                    moved = [
                        jnp.where(below_is_halo, read(theirs, c * sites, at - top), read(halo, c * PLANE, at - top))
                        for c in range(6)
                    ]
                kind = 3 if sign_at == 0 else 2
                value = lambda row, kind=kind, at=at: links[kind, pl.ds(row, 1), pl.ds(at, LANES)]
                link = lambda a, b, value=value: (value((a * 3 + b) * 2), value((a * 3 + b) * 2 + 1))
                store_left(refs[2 + slab], 0, slab, 2, sign_at, at, moved, link, phase_ref, momenta, rows, sites)


def product_kernel(sites, half, first_row, size, parts, pairs, received, targets, *refs):
    mine, theirs = refs[:parts], refs[parts : 2 * parts]
    left = refs[2 * parts : 2 * parts + 2 * pairs]
    got = refs[2 * parts + 2 * pairs : 2 * parts + 2 * pairs + received]
    *outs, right, rows, right_sems, left_sems = refs[2 * parts + 2 * pairs + received :]
    width = right.shape[0] // 2
    span = 6 * sites
    chunks = half * pairs
    columns = [pl.ds(slab * span, span) for slab in range(2)]
    right_copies, left_copies = [[], []], [[], []]
    for slab, pieces in enumerate((mine, theirs)):
        start = 0
        for n, piece in enumerate(pieces):
            count = piece.shape[0]
            right_copies[slab].append(
                pltpu.make_async_copy(piece, right.at[pl.ds(start, count), columns[slab]], right_sems.at[slab, n])
            )
            start += count
        for n in range(chunks):
            left_copies[slab].append(
                pltpu.make_async_copy(
                    left[2 * (n // half) + slab].at[n % half, pl.ds(first_row, size)],
                    rows.at[pl.ds(n * size, size), columns[slab]], left_sems.at[slab, n],
                )
            )
    together = max(1, ROWS // size)
    groups = [range(n, min(n + together, chunks)) for n in range(0, chunks, together)]
    for group in groups:
        for slab in range(2):
            for copy in (right_copies[slab] if group is groups[0] else []) + [left_copies[slab][n] for n in group]:
                copy.start()
    for group in groups:
        sums = None
        here = pl.ds(group[0] * size, len(group) * size)
        for slab in range(2):
            if group is groups[0]:
                for copy in right_copies[slab]:
                    copy.wait()
                for colour in range(3):
                    real_at = slab * span + 2 * colour * sites
                    imag_at = real_at + sites
                    right[pl.ds(width, width), pl.ds(real_at, sites)] = right[pl.ds(0, width), pl.ds(imag_at, sites)]
                    right[pl.ds(width, width), pl.ds(imag_at, sites)] = -right[pl.ds(0, width), pl.ds(real_at, sites)]
            for n in group:
                left_copies[slab][n].wait()
            part = lax.dot_general(
                rows[here, columns[slab]], right[:, columns[slab]], (((1,), (1,)), ((), ())),
                preferred_element_type=jnp.float32,
            )
            sums = part if sums is None else sums + part
        for m, n in enumerate(group):
            which, place = targets[n]
            for q in range(2):
                total = sums[m * size : (m + 1) * size, q * width : (q + 1) * width]
                if not got:
                    outs[which][place, q] = total.astype(outs[which].dtype)
                start = 0
                for ref in got:
                    count = ref.shape[2]
                    added = total[start : start + count] + ref[n, q].astype(jnp.float32)
                    outs[which][place, q, pl.ds(start, count)] = added.astype(outs[which].dtype)
                    start += count


def finish_kernel(pieces, momenta, rows, scale, place_ref, *refs):
    out_ref = refs[-1]
    size = momenta * rows
    for d in range(6):
        at = pl.ds(pl.multiple_of(place_ref[d] * size, size), size)
        for q in range(2):
            total = refs[0][0, q, at].astype(jnp.float32)
            for ref in refs[1:pieces]:
                total = total + ref[0, q, at].astype(jnp.float32)
            total = total * scale
            for p in range(momenta):
                out_ref[d, p, q] = total[p * rows : (p + 1) * rows]


def after(value, *earlier):
    return lax.optimization_barrier((value, *earlier))[0]


def order(last):
    steps = [("left", (1, 0)), ("left", (1, 1)), ("xy", 0), ("halo", 0), ("pass", 1), ("left_z", 1), ("z", 0)]
    steps += [("left", (0, 0)), ("wait", 0), ("pass", 2), ("left", (0, 1)), ("left_z", 0), ("wait", 1)]
    if last > 0:
        steps.append(("away", 1))
    for n in range(last + 1):
        if n + 3 <= last:
            steps.append(("pass", n + 3))
        if n + 2 <= last:
            steps.append(("away", n + 2))
        steps.append(("home", n))
        if n > 1:
            steps.append(("finish", n - 2))
    return steps + [("finish", n) for n in range(max(last - 1, 0), last + 1)]


def on_device(vectors, links, dirs, moms):
    count, sites = vectors.shape[0], vectors.shape[-1]
    momenta = moms.shape[0]
    groups, slabs = lax.axis_size("vec"), lax.axis_size("gz")
    chips = slabs // CORES
    half = chips // 2
    rows = count // slabs
    depth = sites // PLANE
    span = 6 * sites
    group, slab = lax.axis_index("vec"), lax.axis_index("gz")
    core, chip = slab % CORES, slab // CORES
    place = jnp.stack((chip, core)).astype(jnp.int32)
    across = [(i, i ^ 1) for i in range(slabs)]
    params = pltpu.CompilerParams(vmem_limit_bytes=VMEM_BYTES)

    link_rows = links.reshape(3, 18, sites)
    top = link_rows[2, :, sites - PLANE :]
    other_links = lax.ppermute(link_rows, "gz", across)
    below = lax.ppermute(top, "gz", [(i, (i + 1) % slabs) for i in range(slabs)])
    two_below = lax.ppermute(top, "gz", [(i, (i + 2) % slabs) for i in range(slabs)])

    def with_shifted(link, lower):
        moved = jnp.concatenate((lower, link[2, :, : sites - PLANE]), axis=-1)
        return jnp.concatenate((link, moved[None]), axis=0)

    tables = with_shifted(link_rows, below)
    other_tables = with_shifted(other_links, jnp.where(core == 0, top, two_below))

    flat = after(vectors.reshape(count, span), other_links, below, two_below)
    other = lax.ppermute(flat, "gz", across)

    edge = pl.pallas_call(
        functools.partial(edge_kernel, sites),
        grid_spec=pltpu.PrefetchScalarGridSpec(
            num_scalar_prefetch=1,
            grid=(chips,),
            in_specs=[pl.BlockSpec((count // chips, span), lambda n, place: (n, 0))],
            out_specs=pl.BlockSpec((count // chips, 6 * PLANE), lambda n, place: (n, 0)),
        ),
        out_shape=jax.ShapeDtypeStruct((count, 6 * PLANE), jnp.bfloat16),
        compiler_params=params,
        cost_estimate=cost(1e9),
        name="edges",
    )(place, flat)
    step = lambda i: (i - CORES if i % CORES == 0 else i + CORES) % slabs
    halo = {0: lax.ppermute(edge, "gz", [(i, step(i)) for i in range(slabs)])}

    phase_rows = 2 * 3 * 2 * momenta
    phases = pl.pallas_call(
        functools.partial(phase_kernel, momenta, sites, (LX, LY, depth * slabs)),
        in_specs=[pl.BlockSpec(memory_space=pltpu.SMEM)] * 2,
        out_shape=jax.ShapeDtypeStruct((2, phase_rows, sites), jnp.float32),
        scratch_shapes=[pltpu.VMEM((phase_rows, sites), jnp.float32)],
        compiler_params=params,
        cost_estimate=cost(1e9),
        name="phases",
    )(place, moms)

    left_rows = 6 * momenta * rows
    whole = lambda array: pl.BlockSpec(array.shape, lambda n, place: (0,) * array.ndim)
    left_shape = jax.ShapeDtypeStruct((half, left_rows, span), jnp.bfloat16)

    def left_specs(odd):
        mine = lambda n, place: ((place[0] ^ (2 * n + odd)) * CORES + place[1], 0)
        return pl.BlockSpec((rows, span), mine), pl.BlockSpec((rows, 6 * PLANE), mine)

    def left_xy(odd, which, vecs, table, place):
        return pl.pallas_call(
            functools.partial(left_xy_kernel, momenta, rows, sites, which),
            grid_spec=pltpu.PrefetchScalarGridSpec(
                num_scalar_prefetch=1,
                grid=(half,),
                in_specs=[left_specs(odd)[0], whole(table), whole(phases)],
                out_specs=pl.BlockSpec((1, 4 * momenta * rows, span), lambda n, place: (n, 0, 0)),
                scratch_shapes=[pltpu.VMEM((18, PLANE), jnp.float32)],
            ),
            out_shape=left_shape,
            compiler_params=params,
            cost_estimate=cost(4e9 if odd == 0 else 0.5e9),
            name="left_xy",
        )(place, vecs, table, phases)

    def left_z(odd, sides):
        vec_spec, halo_spec = left_specs(odd)
        kept = pl.BlockSpec(memory_space=pl.ANY)
        return pl.pallas_call(
            functools.partial(left_z_kernel, momenta, rows, sites),
            grid_spec=pltpu.PrefetchScalarGridSpec(
                num_scalar_prefetch=1,
                grid=(half,),
                in_specs=[
                    vec_spec, vec_spec, halo_spec, halo_spec, whole(tables), whole(other_tables), whole(phases), kept, kept,
                ],
                out_specs=[pl.BlockSpec((1, 2 * momenta * rows, span), lambda n, place: (n, 2, 0))] * 2,
            ),
            out_shape=[left_shape] * 2,
            input_output_aliases={8: 0, 9: 1},
            compiler_params=params,
            cost_estimate=cost(5e9),
            name="left_z",
        )(place, flat, other, halo[0], halo[1], tables, other_tables, phases, *sides)

    def product(sides, mine, theirs, targets, kinds, first_row=0, size=left_rows, received=(), work=7e9):
        width = sum(piece.shape[0] for piece in mine)
        kept = pl.BlockSpec(memory_space=pl.ANY)
        in_vmem = pl.BlockSpec(memory_space=pltpu.VMEM)
        chunks = [sum(which == n for which, _ in targets) for n in range(len(kinds))]
        pairs = len(sides) // 2
        return pl.pallas_call(
            functools.partial(product_kernel, sites, half, first_row, size, len(mine), pairs, len(received), targets),
            in_specs=[kept] * (2 * len(mine) + len(sides)) + [in_vmem] * len(received),
            out_specs=[in_vmem] * len(kinds),
            out_shape=[jax.ShapeDtypeStruct((n, 2, size, width), kind) for n, kind in zip(chunks, kinds)],
            scratch_shapes=[
                pltpu.VMEM((2 * width, 2 * span), jnp.bfloat16),
                pltpu.VMEM((pairs * half * size, 2 * span), jnp.bfloat16),
                pltpu.SemaphoreType.DMA((2, len(mine))),
                pltpu.SemaphoreType.DMA((2, pairs * half)),
            ],
            compiler_params=params,
            cost_estimate=cost(work),
            name="product",
        )(*mine, *theirs, *sides, *received)

    def product_away(sides, right, first_row, size, work):
        (away,) = product(sides, *right, [(0, n) for n in range(half)], [jnp.bfloat16], first_row, size, work=work)
        return away, to_chip(away, 1)

    def product_home(sides, right, received, work):
        if half == 1:
            return product(sides, *right, [(0, 0)], [jnp.float32], received=received, work=work)
        targets = [(n % 2, n // 2) for n in range(half)]
        return product(sides, *right, targets, [jnp.float32, jnp.bfloat16], received=received, work=work)

    scale = 1.0 / math.sqrt(3.0 * sites * slabs)
    spots = 2 * (dirs % 3) + dirs // 3
    out_shape = jax.ShapeDtypeStruct((6, momenta, 2, rows, groups * count), jnp.float32)

    def finish(pieces, places, result):
        at = jnp.concatenate((spots, jnp.stack(places))).astype(jnp.int32)
        in_specs = [pl.BlockSpec((1, 2, left_rows, LANES), lambda n, at: (0, 0, 0, n))] * len(pieces)
        operands = list(pieces)
        aliases = {}
        if result is not None:
            in_specs.append(pl.BlockSpec(memory_space=pl.ANY))
            operands.append(result)
            aliases = {len(operands): 0}
        return pl.pallas_call(
            functools.partial(finish_kernel, len(pieces), momenta, rows, scale),
            grid_spec=pltpu.PrefetchScalarGridSpec(
                num_scalar_prefetch=1,
                grid=(len(places),),
                in_specs=in_specs,
                out_specs=pl.BlockSpec((6, momenta, 2, rows, LANES), lambda n, at: (0, 0, 0, 0, at[6 + n])),
            ),
            out_shape=out_shape,
            input_output_aliases=aliases,
            compiler_params=params,
            cost_estimate=cost(0.1e9),
            name="finish",
        )(at, *operands)

    def to_chip(array, bit):
        return lax.ppermute(array, "gz", [(i, i ^ (CORES * bit)) for i in range(slabs)])

    def from_group(array, turn):
        return lax.ppermute(array, "vec", [(i, i ^ turn) for i in range(groups)])

    def to_core(arrays):
        return [lax.ppermute(array, "gz", across) for array in arrays]

    def reduce_more(kept, away=None):
        if away is None:
            return [kept]
        pieces, bit = [(kept, 4), (to_chip(away, 2), 4)], 4
        while bit < chips:
            terms = [piece[bit // stride :: 2 * bit // stride].astype(jnp.float32) for piece, stride in pieces]
            away = functools.reduce(jnp.add, terms).astype(jnp.bfloat16)
            pieces.append((to_chip(away, bit), 2 * bit))
            bit *= 2
        return [piece for piece, _ in pieces]

    part = count // 2
    split = groups > 2 and part % LANES == 0
    if split:
        blocks = [[(1, 0), (2, 0)], [(1, 1), (2, 1)], [(3, 0), (3, 1)]] + [[(turn, None)] for turn in range(4, groups)]
    else:
        blocks = [[(turn, None)] for turn in range(1, groups)]
    source = {None: flat, 0: flat[:part], 1: flat[part:]}
    wide = count // LANES

    def columns(block):
        places = []
        for turn, which in block:
            at = (group ^ turn) * wide
            places += [at + n for n in range(wide)] if which is None else [at + which * (wide // 2) + n for n in range(wide // 2)]
        return places

    def fetch(block, *earlier):
        taken = []
        for turn, which in block:
            if split and turn == 3:
                piece, turn = (arriving[1][0], 2) if which == 0 else (arriving[2][1], 1)
            else:
                piece = source[which]
            taken.append(from_group(after(piece, *earlier) if earlier else piece, turn))
        return taken

    def own_columns(n):
        return columns([(0, None)] if n == 0 else blocks[n - 1])

    def pass_on(n, *earlier):
        if n not in arriving:
            return
        mine = [after(array, *earlier) for array in arriving[n]]
        mine = [jnp.concatenate(mine, axis=0)] if len(mine) > 1 else mine
        if n < len(blocks):
            arriving[n + 1] = fetch(blocks[n], *mine)
        right[n] = (mine, to_core(mine))

    last = len(blocks)
    arriving = {1: fetch(blocks[0])} if blocks else {}
    right = {0: ([flat], [other])}
    flat_rows = 4 * momenta * rows
    sides = {1: [None, None], 0: [None, None]}
    received, sums = {0: []}, {}
    done, held, result = place, (), None

    def run(step, n):
        nonlocal done, held, result
        now = (done, *held)
        if step not in ("pass", "halo"):
            held = ()
        if step == "left":
            odd, which = n
            vecs, table = ((flat, tables), (other, other_tables))[which]
            sides[odd][which] = done = left_xy(odd, which, vecs, table, after(place, *now))
        elif step == "left_z":
            sides[n] = left_z(n, [sides[n][0], after(sides[n][1], *now)])
            done = sides[n][0]
        elif step == "pass":
            pass_on(n, *now)
        elif step == "halo":
            halo[1] = lax.ppermute(after(halo[0], *now), "gz", across)
        elif step == "wait":
            held = (received[0][n],)
        elif step == "finish":
            result = done = finish([after(sums[n][0], *now)] + sums[n][1:], own_columns(n), result)
        else:
            even = [after(sides[0][0], *now), sides[0][1]]
            odd = [after(sides[1][0], *now), sides[1][1]]
            if step == "xy":
                done, arrived = product_away(odd, right[n], 0, flat_rows, 1e9)
                received[n].append(arrived)
            elif step == "z":
                done, arrived = product_away(odd, right[n], flat_rows, left_rows - flat_rows, 2.5e9)
                received[n].append(arrived)
            elif step == "away":
                done, arrived = product_away(odd, right[n], 0, left_rows, 5e9)
                received[n] = [arrived]
            elif step == "home":
                outs = product_home(even, right[n], received[n], 4e9 if n < last - 1 else 1e9)
                sums[n], done = reduce_more(*outs), outs[0]

    for step, n in order(last):
        run(step, n)
    return result


def solution(mesh):
    placed = (P("vec", None, None, "gz"), P(None, None, None, None, "gz"), P(), P())
    return jax.shard_map(
        on_device,
        mesh=mesh,
        in_specs=placed,
        out_specs=P(None, None, None, ("vec", "gz"), None),
        check_vma=False,
    )
```

```python
import functools
import math

import jax
import jax.numpy as jnp
from jax import lax
from jax.experimental import pallas as pl
from jax.experimental.pallas import tpu as pltpu
from jax.sharding import PartitionSpec as P

LX = 32
LY = 8
PLANE = LX * LY
LANES = 128
CORES = 2
VMEM_BYTES = 48 * 1024 * 1024
COST_SCALE = 1.0
ROWS = 384


def cost(work):
    return pl.CostEstimate(flops=int(work * COST_SCALE), bytes_accessed=1024, transcendentals=0)


def shifted(chunks, axis, sign):
    lane = lax.broadcasted_iota(jnp.int32, chunks[0].shape, 1)
    if axis == 0:
        near = LANES - 1 if sign > 0 else 1
        far = LX - 1 if sign > 0 else LANES - (LX - 1)
        edge = lax.rem(lane, LX) == (LX - 1 if sign > 0 else 0)
        return [jnp.where(edge, pltpu.roll(c, far, 1), pltpu.roll(c, near, 1)) for c in chunks]
    turned = [pltpu.roll(c, LANES - LX if sign > 0 else LX, 1) for c in chunks]
    inside = lane < LANES - LX if sign > 0 else lane >= LX
    count = len(chunks)
    return [jnp.where(inside, turned[n], turned[(n + sign) % count]) for n in range(count)]


def apply_link(moved, link, adjoint):
    for row in range(3):
        real = imag = None
        for column in range(3):
            link_real, link_imag = link(column, row) if adjoint else link(row, column)
            vec_real, vec_imag = moved[2 * column], moved[2 * column + 1]
            if adjoint:
                terms = (link_real * vec_real + link_imag * vec_imag, link_real * vec_imag - link_imag * vec_real)
            else:
                terms = (link_real * vec_real - link_imag * vec_imag, link_real * vec_imag + link_imag * vec_real)
            real, imag = terms if real is None else (real + terms[0], imag + terms[1])
        yield row, real, imag


def store_left(out_ref, base, slab, axis, sign_at, first, moved, link, phase_ref, momenta, rows, sites):
    lanes = pl.ds(first, LANES)
    for row, real, imag in apply_link(moved, link, sign_at == 0):
        for p in range(momenta):
            at = ((slab * 3 + axis) * 2 + sign_at) * momenta + p
            cosine = phase_ref[0, pl.ds(at, 1), lanes]
            sine = phase_ref[1, pl.ds(at, 1), lanes]
            down = pl.ds(base + (sign_at * momenta + p) * rows, rows)
            column = row * 2 * sites + first
            out_ref[0, down, pl.ds(column, LANES)] = (cosine * real - sine * imag).astype(jnp.bfloat16)
            out_ref[0, down, pl.ds(column + sites, LANES)] = (sine * real + cosine * imag).astype(jnp.bfloat16)


def phase_kernel(momenta, sites, extents, place_ref, moms_ref, out_ref, angles):
    flat = lax.broadcasted_iota(jnp.int32, (1, sites), 1)
    depth = sites // PLANE
    turns = [[moms_ref[p, mu].astype(jnp.float32) / extents[mu] for mu in range(3)] for p in range(momenta)]
    at = 0
    for slab in range(2):
        core = place_ref[1] if slab == 0 else 1 - place_ref[1]
        planes = flat // PLANE + (place_ref[0] * CORES + core) * depth
        coordinates = [c.astype(jnp.float32) for c in (lax.rem(flat, LX), lax.rem(flat // LX, LY), planes)]
        base = [sum(turns[p][mu] * coordinates[mu] for mu in range(3)) for p in range(momenta)]
        for axis in range(3):
            for sign in (-1.0, 1.0):
                for p in range(momenta):
                    angles[pl.ds(at, 1), :] = (base[p] + sign * turns[p][axis]) * (2.0 * math.pi)
                    at += 1
    out_ref[0] = jnp.cos(angles[...])
    out_ref[1] = jnp.sin(angles[...])


def edge_kernel(sites, place_ref, vec_ref, out_ref):
    for c in range(6):
        lowest = vec_ref[:, pl.ds(c * sites, PLANE)]
        highest = vec_ref[:, pl.ds((c + 1) * sites - PLANE, PLANE)]
        out_ref[:, pl.ds(c * PLANE, PLANE)] = jnp.where(place_ref[1] == 0, lowest, highest)


def left_xy_kernel(momenta, rows, sites, slab, place_ref, vec_ref, link_ref, phase_ref, out_ref, table):
    chunks = PLANE // LANES
    for axis in range(2):
        for plane in range(sites // PLANE):
            starts = [plane * PLANE + n * LANES for n in range(chunks)]
            behind = shifted([link_ref[axis, :, pl.ds(at, LANES)] for at in starts], axis, -1)
            for n in range(chunks):
                table[:, pl.ds(n * LANES, LANES)] = behind[n]
            parts = [[vec_ref[:, pl.ds(c * sites + at, LANES)].astype(jnp.float32) for at in starts] for c in range(6)]
            for sign_at, sign in enumerate((-1, 1)):
                moved = [shifted(part, axis, sign) for part in parts]
                for n, at in enumerate(starts):
                    if sign_at == 0:
                        source = lambda row, n=n: table[pl.ds(row, 1), pl.ds(n * LANES, LANES)]
                    else:
                        source = lambda row, at=at: link_ref[axis, pl.ds(row, 1), pl.ds(at, LANES)]
                    link = lambda a, b, source=source: (source((a * 3 + b) * 2), source((a * 3 + b) * 2 + 1))
                    store_left(
                        out_ref, axis * 2 * momenta * rows, slab, axis, sign_at, at, [m[n] for m in moved], link,
                        phase_ref, momenta, rows, sites,
                    )


def left_z_kernel(
    momenta, rows, sites, place_ref, own_ref, other_ref, first_ref, second_ref, link_ref, other_link_ref, phase_ref,
    *refs,
):
    low = place_ref[1] == 0
    top = sites - PLANE
    read = lambda ref, c, at: ref[:, pl.ds(c + at, LANES)].astype(jnp.float32)
    for slab in range(2):
        mine, theirs = (own_ref, other_ref) if slab == 0 else (other_ref, own_ref)
        links = link_ref if slab == 0 else other_link_ref
        below_is_halo = low if slab == 0 else jnp.logical_not(low)
        halo = second_ref if slab == 0 else first_ref
        for at in range(0, sites, LANES):
            for sign_at, sign in enumerate((-1, 1)):
                source = at + sign * PLANE
                if 0 <= source < sites:
                    moved = [read(mine, c * sites, source) for c in range(6)]
                elif source < 0:
                    moved = [
                        jnp.where(below_is_halo, read(halo, c * PLANE, at), read(theirs, c * sites, top + at))
                        for c in range(6)
                    ]
                else:
                    moved = [
                        jnp.where(below_is_halo, read(theirs, c * sites, at - top), read(halo, c * PLANE, at - top))
                        for c in range(6)
                    ]
                kind = 3 if sign_at == 0 else 2
                value = lambda row, kind=kind, at=at: links[kind, pl.ds(row, 1), pl.ds(at, LANES)]
                link = lambda a, b, value=value: (value((a * 3 + b) * 2), value((a * 3 + b) * 2 + 1))
                store_left(refs[2 + slab], 0, slab, 2, sign_at, at, moved, link, phase_ref, momenta, rows, sites)


def product_kernel(sites, half, first_row, size, parts, pairs, received, targets, *refs):
    mine, theirs = refs[:parts], refs[parts : 2 * parts]
    left = refs[2 * parts : 2 * parts + 2 * pairs]
    got = refs[2 * parts + 2 * pairs : 2 * parts + 2 * pairs + received]
    *outs, right, rows, right_sems, left_sems = refs[2 * parts + 2 * pairs + received :]
    width = right.shape[0] // 2
    span = 6 * sites
    chunks = half * pairs
    columns = [pl.ds(slab * span, span) for slab in range(2)]
    right_copies, left_copies = [[], []], [[], []]
    for slab, pieces in enumerate((mine, theirs)):
        start = 0
        for n, piece in enumerate(pieces):
            count = piece.shape[0]
            right_copies[slab].append(
                pltpu.make_async_copy(piece, right.at[pl.ds(start, count), columns[slab]], right_sems.at[slab, n])
            )
            start += count
        for n in range(chunks):
            left_copies[slab].append(
                pltpu.make_async_copy(
                    left[2 * (n // half) + slab].at[n % half, pl.ds(first_row, size)],
                    rows.at[pl.ds(n * size, size), columns[slab]], left_sems.at[slab, n],
                )
            )
    together = max(1, ROWS // size)
    groups = [range(n, min(n + together, chunks)) for n in range(0, chunks, together)]
    for group in groups:
        for slab in range(2):
            for copy in (right_copies[slab] if group is groups[0] else []) + [left_copies[slab][n] for n in group]:
                copy.start()
    for group in groups:
        sums = None
        here = pl.ds(group[0] * size, len(group) * size)
        for slab in range(2):
            if group is groups[0]:
                for copy in right_copies[slab]:
                    copy.wait()
                for colour in range(3):
                    real_at = slab * span + 2 * colour * sites
                    imag_at = real_at + sites
                    right[pl.ds(width, width), pl.ds(real_at, sites)] = right[pl.ds(0, width), pl.ds(imag_at, sites)]
                    right[pl.ds(width, width), pl.ds(imag_at, sites)] = -right[pl.ds(0, width), pl.ds(real_at, sites)]
            for n in group:
                left_copies[slab][n].wait()
            part = lax.dot_general(
                rows[here, columns[slab]], right[:, columns[slab]], (((1,), (1,)), ((), ())),
                preferred_element_type=jnp.float32,
            )
            sums = part if sums is None else sums + part
        for m, n in enumerate(group):
            which, place = targets[n]
            for q in range(2):
                total = sums[m * size : (m + 1) * size, q * width : (q + 1) * width]
                if not got:
                    outs[which][place, q] = total.astype(outs[which].dtype)
                start = 0
                for ref in got:
                    count = ref.shape[2]
                    added = total[start : start + count] + ref[n, q].astype(jnp.float32)
                    outs[which][place, q, pl.ds(start, count)] = added.astype(outs[which].dtype)
                    start += count


def finish_kernel(pieces, momenta, rows, scale, place_ref, *refs):
    out_ref = refs[-1]
    size = momenta * rows
    for d in range(6):
        at = pl.ds(pl.multiple_of(place_ref[d] * size, size), size)
        for q in range(2):
            total = refs[0][0, q, at].astype(jnp.float32)
            for ref in refs[1:pieces]:
                total = total + ref[0, q, at].astype(jnp.float32)
            total = total * scale
            for p in range(momenta):
                out_ref[d, p, q] = total[p * rows : (p + 1) * rows]


def after(value, *earlier):
    return lax.optimization_barrier((value, *earlier))[0]


def order(last):
    steps = [("left", (1, 0)), ("left", (1, 1)), ("xy", 0), ("halo", 0), ("pass", 1), ("left_z", 1), ("z", 0)]
    steps += [("left", (0, 0)), ("wait", 0), ("pass", 2), ("left", (0, 1)), ("left_z", 0), ("wait", 1)]
    if last > 0:
        steps.append(("away", 1))
    for n in range(last + 1):
        if n + 3 <= last:
            steps.append(("pass", n + 3))
        if n + 2 <= last:
            steps.append(("away", n + 2))
        steps.append(("home", n))
        if n > 0:
            steps.append(("finish", n - 1))
    return steps + [("finish", last)]


def on_device(vectors, links, dirs, moms):
    count, sites = vectors.shape[0], vectors.shape[-1]
    momenta = moms.shape[0]
    groups, slabs = lax.axis_size("vec"), lax.axis_size("gz")
    chips = slabs // CORES
    half = chips // 2
    rows = count // slabs
    depth = sites // PLANE
    span = 6 * sites
    group, slab = lax.axis_index("vec"), lax.axis_index("gz")
    core, chip = slab % CORES, slab // CORES
    place = jnp.stack((chip, core)).astype(jnp.int32)
    across = [(i, i ^ 1) for i in range(slabs)]
    params = pltpu.CompilerParams(vmem_limit_bytes=VMEM_BYTES)

    link_rows = links.reshape(3, 18, sites)
    top = link_rows[2, :, sites - PLANE :]
    other_links = lax.ppermute(link_rows, "gz", across)
    below = lax.ppermute(top, "gz", [(i, (i + 1) % slabs) for i in range(slabs)])
    two_below = lax.ppermute(top, "gz", [(i, (i + 2) % slabs) for i in range(slabs)])

    def with_shifted(link, lower):
        moved = jnp.concatenate((lower, link[2, :, : sites - PLANE]), axis=-1)
        return jnp.concatenate((link, moved[None]), axis=0)

    tables = with_shifted(link_rows, below)
    other_tables = with_shifted(other_links, jnp.where(core == 0, top, two_below))

    flat = after(vectors.reshape(count, span), other_links, below, two_below)
    other = lax.ppermute(flat, "gz", across)

    edge = pl.pallas_call(
        functools.partial(edge_kernel, sites),
        grid_spec=pltpu.PrefetchScalarGridSpec(
            num_scalar_prefetch=1,
            grid=(chips,),
            in_specs=[pl.BlockSpec((count // chips, span), lambda n, place: (n, 0))],
            out_specs=pl.BlockSpec((count // chips, 6 * PLANE), lambda n, place: (n, 0)),
        ),
        out_shape=jax.ShapeDtypeStruct((count, 6 * PLANE), jnp.bfloat16),
        compiler_params=params,
        cost_estimate=cost(1e9),
        name="edges",
    )(place, flat)
    step = lambda i: (i - CORES if i % CORES == 0 else i + CORES) % slabs
    halo = {0: lax.ppermute(edge, "gz", [(i, step(i)) for i in range(slabs)])}

    phase_rows = 2 * 3 * 2 * momenta
    phases = pl.pallas_call(
        functools.partial(phase_kernel, momenta, sites, (LX, LY, depth * slabs)),
        in_specs=[pl.BlockSpec(memory_space=pltpu.SMEM)] * 2,
        out_shape=jax.ShapeDtypeStruct((2, phase_rows, sites), jnp.float32),
        scratch_shapes=[pltpu.VMEM((phase_rows, sites), jnp.float32)],
        compiler_params=params,
        cost_estimate=cost(1e9),
        name="phases",
    )(place, moms)

    left_rows = 6 * momenta * rows
    whole = lambda array: pl.BlockSpec(array.shape, lambda n, place: (0,) * array.ndim)
    left_shape = jax.ShapeDtypeStruct((half, left_rows, span), jnp.bfloat16)

    def left_specs(odd):
        mine = lambda n, place: ((place[0] ^ (2 * n + odd)) * CORES + place[1], 0)
        return pl.BlockSpec((rows, span), mine), pl.BlockSpec((rows, 6 * PLANE), mine)

    def left_xy(odd, which, vecs, table, place):
        return pl.pallas_call(
            functools.partial(left_xy_kernel, momenta, rows, sites, which),
            grid_spec=pltpu.PrefetchScalarGridSpec(
                num_scalar_prefetch=1,
                grid=(half,),
                in_specs=[left_specs(odd)[0], whole(table), whole(phases)],
                out_specs=pl.BlockSpec((1, 4 * momenta * rows, span), lambda n, place: (n, 0, 0)),
                scratch_shapes=[pltpu.VMEM((18, PLANE), jnp.float32)],
            ),
            out_shape=left_shape,
            compiler_params=params,
            cost_estimate=cost(4e9 if odd == 0 else 0.5e9),
            name="left_xy",
        )(place, vecs, table, phases)

    def left_z(odd, sides):
        vec_spec, halo_spec = left_specs(odd)
        kept = pl.BlockSpec(memory_space=pl.ANY)
        return pl.pallas_call(
            functools.partial(left_z_kernel, momenta, rows, sites),
            grid_spec=pltpu.PrefetchScalarGridSpec(
                num_scalar_prefetch=1,
                grid=(half,),
                in_specs=[
                    vec_spec, vec_spec, halo_spec, halo_spec, whole(tables), whole(other_tables), whole(phases), kept, kept,
                ],
                out_specs=[pl.BlockSpec((1, 2 * momenta * rows, span), lambda n, place: (n, 2, 0))] * 2,
            ),
            out_shape=[left_shape] * 2,
            input_output_aliases={8: 0, 9: 1},
            compiler_params=params,
            cost_estimate=cost(5e9),
            name="left_z",
        )(place, flat, other, halo[0], halo[1], tables, other_tables, phases, *sides)

    def product(sides, mine, theirs, targets, kinds, first_row=0, size=left_rows, received=(), work=7e9):
        width = sum(piece.shape[0] for piece in mine)
        kept = pl.BlockSpec(memory_space=pl.ANY)
        in_vmem = pl.BlockSpec(memory_space=pltpu.VMEM)
        chunks = [sum(which == n for which, _ in targets) for n in range(len(kinds))]
        pairs = len(sides) // 2
        return pl.pallas_call(
            functools.partial(product_kernel, sites, half, first_row, size, len(mine), pairs, len(received), targets),
            in_specs=[kept] * (2 * len(mine) + len(sides)) + [in_vmem] * len(received),
            out_specs=[in_vmem] * len(kinds),
            out_shape=[jax.ShapeDtypeStruct((n, 2, size, width), kind) for n, kind in zip(chunks, kinds)],
            scratch_shapes=[
                pltpu.VMEM((2 * width, 2 * span), jnp.bfloat16),
                pltpu.VMEM((pairs * half * size, 2 * span), jnp.bfloat16),
                pltpu.SemaphoreType.DMA((2, len(mine))),
                pltpu.SemaphoreType.DMA((2, pairs * half)),
            ],
            compiler_params=params,
            cost_estimate=cost(work),
            name="product",
        )(*mine, *theirs, *sides, *received)

    def product_away(sides, right, first_row, size, work):
        (away,) = product(sides, *right, [(0, n) for n in range(half)], [jnp.bfloat16], first_row, size, work=work)
        return away, to_chip(away, 1)

    def product_home(sides, right, received, work):
        if half == 1:
            return product(sides, *right, [(0, 0)], [jnp.float32], received=received, work=work)
        targets = [(n % 2, n // 2) for n in range(half)]
        return product(sides, *right, targets, [jnp.float32, jnp.bfloat16], received=received, work=work)

    scale = 1.0 / math.sqrt(3.0 * sites * slabs)
    spots = 2 * (dirs % 3) + dirs // 3
    out_shape = jax.ShapeDtypeStruct((6, momenta, 2, rows, groups * count), jnp.float32)

    def finish(pieces, places, result):
        at = jnp.concatenate((spots, jnp.stack(places))).astype(jnp.int32)
        in_specs = [pl.BlockSpec((1, 2, left_rows, LANES), lambda n, at: (0, 0, 0, n))] * len(pieces)
        operands = list(pieces)
        aliases = {}
        if result is not None:
            in_specs.append(pl.BlockSpec(memory_space=pl.ANY))
            operands.append(result)
            aliases = {len(operands): 0}
        return pl.pallas_call(
            functools.partial(finish_kernel, len(pieces), momenta, rows, scale),
            grid_spec=pltpu.PrefetchScalarGridSpec(
                num_scalar_prefetch=1,
                grid=(len(places),),
                in_specs=in_specs,
                out_specs=pl.BlockSpec((6, momenta, 2, rows, LANES), lambda n, at: (0, 0, 0, 0, at[6 + n])),
            ),
            out_shape=out_shape,
            input_output_aliases=aliases,
            compiler_params=params,
            cost_estimate=cost(0.1e9),
            name="finish",
        )(at, *operands)

    def to_chip(array, bit):
        return lax.ppermute(array, "gz", [(i, i ^ (CORES * bit)) for i in range(slabs)])

    def from_group(array, turn):
        return lax.ppermute(array, "vec", [(i, i ^ turn) for i in range(groups)])

    def to_core(arrays):
        return [lax.ppermute(array, "gz", across) for array in arrays]

    def reduce_more(kept, away=None):
        if away is None:
            return [kept]
        pieces, bit = [(kept, 4), (to_chip(away, 2), 4)], 4
        while bit < chips:
            terms = [piece[bit // stride :: 2 * bit // stride].astype(jnp.float32) for piece, stride in pieces]
            away = functools.reduce(jnp.add, terms).astype(jnp.bfloat16)
            pieces.append((to_chip(away, bit), 2 * bit))
            bit *= 2
        return [piece for piece, _ in pieces]

    part = count // 2
    split = groups > 2 and part % LANES == 0
    if split:
        blocks = [[(1, 0), (2, 0)], [(1, 1), (2, 1)], [(3, 0), (3, 1)]] + [[(turn, None)] for turn in range(4, groups)]
    else:
        blocks = [[(turn, None)] for turn in range(1, groups)]
    source = {None: flat, 0: flat[:part], 1: flat[part:]}
    wide = count // LANES

    def columns(block):
        places = []
        for turn, which in block:
            at = (group ^ turn) * wide
            places += [at + n for n in range(wide)] if which is None else [at + which * (wide // 2) + n for n in range(wide // 2)]
        return places

    def fetch(block, *earlier):
        taken = []
        for turn, which in block:
            if split and turn == 3:
                piece, turn = (arriving[1][0], 2) if which == 0 else (arriving[2][1], 1)
            else:
                piece = source[which]
            taken.append(from_group(after(piece, *earlier) if earlier else piece, turn))
        return taken

    def own_columns(n):
        return columns([(0, None)] if n == 0 else blocks[n - 1])

    def pass_on(n, *earlier):
        if n not in arriving:
            return
        mine = [after(array, *earlier) for array in arriving[n]]
        mine = [jnp.concatenate(mine, axis=0)] if len(mine) > 1 else mine
        if n < len(blocks):
            arriving[n + 1] = fetch(blocks[n], *mine)
        right[n] = (mine, to_core(mine))

    last = len(blocks)
    arriving = {1: fetch(blocks[0])} if blocks else {}
    right = {0: ([flat], [other])}
    flat_rows = 4 * momenta * rows
    sides = {1: [None, None], 0: [None, None]}
    received, sums = {0: []}, {}
    done, held, result = place, (), None

    def run(step, n):
        nonlocal done, held, result
        now = (done, *held)
        if step not in ("pass", "halo"):
            held = ()
        if step == "left":
            odd, which = n
            vecs, table = ((flat, tables), (other, other_tables))[which]
            sides[odd][which] = done = left_xy(odd, which, vecs, table, after(place, *now))
        elif step == "left_z":
            sides[n] = left_z(n, [sides[n][0], after(sides[n][1], *now)])
            done = sides[n][0]
        elif step == "pass":
            pass_on(n, *now)
        elif step == "halo":
            halo[1] = lax.ppermute(after(halo[0], *now), "gz", across)
        elif step == "wait":
            held = (received[0][n],)
        elif step == "finish":
            result = done = finish([after(sums[n][0], *now)] + sums[n][1:], own_columns(n), result)
        else:
            even = [after(sides[0][0], *now), sides[0][1]]
            odd = [after(sides[1][0], *now), sides[1][1]]
            if step == "xy":
                done, arrived = product_away(odd, right[n], 0, flat_rows, 1e9)
                received[n].append(arrived)
            elif step == "z":
                done, arrived = product_away(odd, right[n], flat_rows, left_rows - flat_rows, 2.5e9)
                received[n].append(arrived)
            elif step == "away":
                done, arrived = product_away(odd, right[n], 0, left_rows, 5e9)
                received[n] = [arrived]
            elif step == "home":
                outs = product_home(even, right[n], received[n], 4e9)
                sums[n], done = reduce_more(*outs), outs[0]

    for step, n in order(last):
        run(step, n)
    return result


def solution(mesh):
    placed = (P("vec", None, None, "gz"), P(None, None, None, None, "gz"), P(), P())
    return jax.shard_map(
        on_device,
        mesh=mesh,
        in_specs=placed,
        out_specs=P(None, None, None, ("vec", "gz"), None),
        check_vma=False,
    )
```

```python
import functools
import math

import jax
import jax.numpy as jnp
from jax import lax
from jax.experimental import pallas as pl
from jax.experimental.pallas import tpu as pltpu
from jax.sharding import PartitionSpec as P

LX = 32
LY = 8
PLANE = LX * LY
LANES = 128
CORES = 2
VMEM_BYTES = 48 * 1024 * 1024
COST_SCALE = 1.0
ROWS = 384


def cost(work):
    return pl.CostEstimate(flops=int(work * COST_SCALE), bytes_accessed=1024, transcendentals=0)


def shifted(chunks, axis, sign):
    lane = lax.broadcasted_iota(jnp.int32, chunks[0].shape, 1)
    if axis == 0:
        near = LANES - 1 if sign > 0 else 1
        far = LX - 1 if sign > 0 else LANES - (LX - 1)
        edge = lax.rem(lane, LX) == (LX - 1 if sign > 0 else 0)
        return [jnp.where(edge, pltpu.roll(c, far, 1), pltpu.roll(c, near, 1)) for c in chunks]
    turned = [pltpu.roll(c, LANES - LX if sign > 0 else LX, 1) for c in chunks]
    inside = lane < LANES - LX if sign > 0 else lane >= LX
    count = len(chunks)
    return [jnp.where(inside, turned[n], turned[(n + sign) % count]) for n in range(count)]


def apply_link(moved, link, adjoint):
    for row in range(3):
        real = imag = None
        for column in range(3):
            link_real, link_imag = link(column, row) if adjoint else link(row, column)
            vec_real, vec_imag = moved[2 * column], moved[2 * column + 1]
            if adjoint:
                terms = (link_real * vec_real + link_imag * vec_imag, link_real * vec_imag - link_imag * vec_real)
            else:
                terms = (link_real * vec_real - link_imag * vec_imag, link_real * vec_imag + link_imag * vec_real)
            real, imag = terms if real is None else (real + terms[0], imag + terms[1])
        yield row, real, imag


def store_left(out_ref, base, slab, axis, sign_at, first, moved, link, phase_ref, momenta, rows, sites):
    lanes = pl.ds(first, LANES)
    for row, real, imag in apply_link(moved, link, sign_at == 0):
        for p in range(momenta):
            at = ((slab * 3 + axis) * 2 + sign_at) * momenta + p
            cosine = phase_ref[0, pl.ds(at, 1), lanes]
            sine = phase_ref[1, pl.ds(at, 1), lanes]
            down = pl.ds(base + (sign_at * momenta + p) * rows, rows)
            column = row * 2 * sites + first
            out_ref[0, down, pl.ds(column, LANES)] = (cosine * real - sine * imag).astype(jnp.bfloat16)
            out_ref[0, down, pl.ds(column + sites, LANES)] = (sine * real + cosine * imag).astype(jnp.bfloat16)


def phase_kernel(momenta, sites, extents, place_ref, moms_ref, out_ref, angles):
    flat = lax.broadcasted_iota(jnp.int32, (1, sites), 1)
    depth = sites // PLANE
    turns = [[moms_ref[p, mu].astype(jnp.float32) / extents[mu] for mu in range(3)] for p in range(momenta)]
    at = 0
    for slab in range(2):
        core = place_ref[1] if slab == 0 else 1 - place_ref[1]
        planes = flat // PLANE + (place_ref[0] * CORES + core) * depth
        coordinates = [c.astype(jnp.float32) for c in (lax.rem(flat, LX), lax.rem(flat // LX, LY), planes)]
        base = [sum(turns[p][mu] * coordinates[mu] for mu in range(3)) for p in range(momenta)]
        for axis in range(3):
            for sign in (-1.0, 1.0):
                for p in range(momenta):
                    angles[pl.ds(at, 1), :] = (base[p] + sign * turns[p][axis]) * (2.0 * math.pi)
                    at += 1
    out_ref[0] = jnp.cos(angles[...])
    out_ref[1] = jnp.sin(angles[...])


def edge_kernel(sites, place_ref, vec_ref, out_ref):
    for c in range(6):
        lowest = vec_ref[:, pl.ds(c * sites, PLANE)]
        highest = vec_ref[:, pl.ds((c + 1) * sites - PLANE, PLANE)]
        out_ref[:, pl.ds(c * PLANE, PLANE)] = jnp.where(place_ref[1] == 0, lowest, highest)


def left_xy_kernel(momenta, rows, sites, slab, place_ref, vec_ref, link_ref, phase_ref, out_ref, table):
    chunks = PLANE // LANES
    for axis in range(2):
        for plane in range(sites // PLANE):
            starts = [plane * PLANE + n * LANES for n in range(chunks)]
            behind = shifted([link_ref[axis, :, pl.ds(at, LANES)] for at in starts], axis, -1)
            for n in range(chunks):
                table[:, pl.ds(n * LANES, LANES)] = behind[n]
            parts = [[vec_ref[:, pl.ds(c * sites + at, LANES)].astype(jnp.float32) for at in starts] for c in range(6)]
            for sign_at, sign in enumerate((-1, 1)):
                moved = [shifted(part, axis, sign) for part in parts]
                for n, at in enumerate(starts):
                    if sign_at == 0:
                        source = lambda row, n=n: table[pl.ds(row, 1), pl.ds(n * LANES, LANES)]
                    else:
                        source = lambda row, at=at: link_ref[axis, pl.ds(row, 1), pl.ds(at, LANES)]
                    link = lambda a, b, source=source: (source((a * 3 + b) * 2), source((a * 3 + b) * 2 + 1))
                    store_left(
                        out_ref, axis * 2 * momenta * rows, slab, axis, sign_at, at, [m[n] for m in moved], link,
                        phase_ref, momenta, rows, sites,
                    )


def left_z_kernel(
    momenta, rows, sites, place_ref, own_ref, other_ref, first_ref, second_ref, link_ref, other_link_ref, phase_ref,
    *refs,
):
    low = place_ref[1] == 0
    top = sites - PLANE
    read = lambda ref, c, at: ref[:, pl.ds(c + at, LANES)].astype(jnp.float32)
    for slab in range(2):
        mine, theirs = (own_ref, other_ref) if slab == 0 else (other_ref, own_ref)
        links = link_ref if slab == 0 else other_link_ref
        below_is_halo = low if slab == 0 else jnp.logical_not(low)
        halo = second_ref if slab == 0 else first_ref
        for at in range(0, sites, LANES):
            for sign_at, sign in enumerate((-1, 1)):
                source = at + sign * PLANE
                if 0 <= source < sites:
                    moved = [read(mine, c * sites, source) for c in range(6)]
                elif source < 0:
                    moved = [
                        jnp.where(below_is_halo, read(halo, c * PLANE, at), read(theirs, c * sites, top + at))
                        for c in range(6)
                    ]
                else:
                    moved = [
                        jnp.where(below_is_halo, read(theirs, c * sites, at - top), read(halo, c * PLANE, at - top))
                        for c in range(6)
                    ]
                kind = 3 if sign_at == 0 else 2
                value = lambda row, kind=kind, at=at: links[kind, pl.ds(row, 1), pl.ds(at, LANES)]
                link = lambda a, b, value=value: (value((a * 3 + b) * 2), value((a * 3 + b) * 2 + 1))
                store_left(refs[2 + slab], 0, slab, 2, sign_at, at, moved, link, phase_ref, momenta, rows, sites)


def product_kernel(sites, half, first_row, size, parts, pairs, received, targets, *refs):
    mine, theirs = refs[:parts], refs[parts : 2 * parts]
    left = refs[2 * parts : 2 * parts + 2 * pairs]
    got = refs[2 * parts + 2 * pairs : 2 * parts + 2 * pairs + received]
    *outs, right, rows, right_sems, left_sems = refs[2 * parts + 2 * pairs + received :]
    width = right.shape[0] // 2
    span = 6 * sites
    chunks = half * pairs
    columns = [pl.ds(slab * span, span) for slab in range(2)]
    right_copies, left_copies = [[], []], [[], []]
    for slab, pieces in enumerate((mine, theirs)):
        start = 0
        for n, piece in enumerate(pieces):
            count = piece.shape[0]
            right_copies[slab].append(
                pltpu.make_async_copy(piece, right.at[pl.ds(start, count), columns[slab]], right_sems.at[slab, n])
            )
            start += count
        for n in range(chunks):
            left_copies[slab].append(
                pltpu.make_async_copy(
                    left[2 * (n // half) + slab].at[n % half, pl.ds(first_row, size)],
                    rows.at[pl.ds(n * size, size), columns[slab]], left_sems.at[slab, n],
                )
            )
    together = max(1, ROWS // size)
    groups = [range(n, min(n + together, chunks)) for n in range(0, chunks, together)]
    for group in groups:
        for slab in range(2):
            for copy in (right_copies[slab] if group is groups[0] else []) + [left_copies[slab][n] for n in group]:
                copy.start()
    for group in groups:
        sums = None
        here = pl.ds(group[0] * size, len(group) * size)
        for slab in range(2):
            if group is groups[0]:
                for copy in right_copies[slab]:
                    copy.wait()
                for colour in range(3):
                    real_at = slab * span + 2 * colour * sites
                    imag_at = real_at + sites
                    right[pl.ds(width, width), pl.ds(real_at, sites)] = right[pl.ds(0, width), pl.ds(imag_at, sites)]
                    right[pl.ds(width, width), pl.ds(imag_at, sites)] = -right[pl.ds(0, width), pl.ds(real_at, sites)]
            for n in group:
                left_copies[slab][n].wait()
            part = lax.dot_general(
                rows[here, columns[slab]], right[:, columns[slab]], (((1,), (1,)), ((), ())),
                preferred_element_type=jnp.float32,
            )
            sums = part if sums is None else sums + part
        for m, n in enumerate(group):
            which, place = targets[n]
            for q in range(2):
                total = sums[m * size : (m + 1) * size, q * width : (q + 1) * width]
                if not got:
                    outs[which][place, q] = total.astype(outs[which].dtype)
                start = 0
                for ref in got:
                    count = ref.shape[2]
                    added = total[start : start + count] + ref[n, q].astype(jnp.float32)
                    outs[which][place, q, pl.ds(start, count)] = added.astype(outs[which].dtype)
                    start += count


def finish_kernel(pieces, momenta, rows, scale, place_ref, *refs):
    out_ref = refs[-1]
    size = momenta * rows
    for d in range(6):
        at = pl.ds(pl.multiple_of(place_ref[d] * size, size), size)
        for q in range(2):
            total = refs[0][0, q, at].astype(jnp.float32)
            for ref in refs[1:pieces]:
                total = total + ref[0, q, at].astype(jnp.float32)
            total = total * scale
            for p in range(momenta):
                out_ref[d, p, q] = total[p * rows : (p + 1) * rows]


def after(value, *earlier):
    return lax.optimization_barrier((value, *earlier))[0]


def order(last):
    steps = [("left", (1, 0)), ("left", (1, 1)), ("xy", 0), ("halo", 0), ("pass", 1), ("left_z", 1), ("z", 0)]
    steps += [("left", (0, 0)), ("wait", 0), ("pass", 2), ("left", (0, 1)), ("left_z", 0), ("home", 0)]
    for n in range(1, last + 1):
        steps.append(("away", n))
        if n + 2 <= last:
            steps.append(("pass", n + 2))
    if last > 1:
        steps.append(("wait", 2))
    for n in range(1, last + 1):
        steps += [("home", n), ("finish", n - 1)]
    return steps + [("finish", last)]


def on_device(vectors, links, dirs, moms):
    count, sites = vectors.shape[0], vectors.shape[-1]
    momenta = moms.shape[0]
    groups, slabs = lax.axis_size("vec"), lax.axis_size("gz")
    chips = slabs // CORES
    half = chips // 2
    rows = count // slabs
    depth = sites // PLANE
    span = 6 * sites
    group, slab = lax.axis_index("vec"), lax.axis_index("gz")
    core, chip = slab % CORES, slab // CORES
    place = jnp.stack((chip, core)).astype(jnp.int32)
    across = [(i, i ^ 1) for i in range(slabs)]
    params = pltpu.CompilerParams(vmem_limit_bytes=VMEM_BYTES)

    link_rows = links.reshape(3, 18, sites)
    top = link_rows[2, :, sites - PLANE :]
    other_links = lax.ppermute(link_rows, "gz", across)
    below = lax.ppermute(top, "gz", [(i, (i + 1) % slabs) for i in range(slabs)])
    two_below = lax.ppermute(top, "gz", [(i, (i + 2) % slabs) for i in range(slabs)])

    def with_shifted(link, lower):
        moved = jnp.concatenate((lower, link[2, :, : sites - PLANE]), axis=-1)
        return jnp.concatenate((link, moved[None]), axis=0)

    tables = with_shifted(link_rows, below)
    other_tables = with_shifted(other_links, jnp.where(core == 0, top, two_below))

    flat = after(vectors.reshape(count, span), other_links, below, two_below)
    other = lax.ppermute(flat, "gz", across)

    edge = pl.pallas_call(
        functools.partial(edge_kernel, sites),
        grid_spec=pltpu.PrefetchScalarGridSpec(
            num_scalar_prefetch=1,
            grid=(chips,),
            in_specs=[pl.BlockSpec((count // chips, span), lambda n, place: (n, 0))],
            out_specs=pl.BlockSpec((count // chips, 6 * PLANE), lambda n, place: (n, 0)),
        ),
        out_shape=jax.ShapeDtypeStruct((count, 6 * PLANE), jnp.bfloat16),
        compiler_params=params,
        cost_estimate=cost(1e9),
        name="edges",
    )(place, flat)
    step = lambda i: (i - CORES if i % CORES == 0 else i + CORES) % slabs
    halo = {0: lax.ppermute(edge, "gz", [(i, step(i)) for i in range(slabs)])}

    phase_rows = 2 * 3 * 2 * momenta
    phases = pl.pallas_call(
        functools.partial(phase_kernel, momenta, sites, (LX, LY, depth * slabs)),
        in_specs=[pl.BlockSpec(memory_space=pltpu.SMEM)] * 2,
        out_shape=jax.ShapeDtypeStruct((2, phase_rows, sites), jnp.float32),
        scratch_shapes=[pltpu.VMEM((phase_rows, sites), jnp.float32)],
        compiler_params=params,
        cost_estimate=cost(1e9),
        name="phases",
    )(place, moms)

    left_rows = 6 * momenta * rows
    whole = lambda array: pl.BlockSpec(array.shape, lambda n, place: (0,) * array.ndim)
    left_shape = jax.ShapeDtypeStruct((half, left_rows, span), jnp.bfloat16)

    def left_specs(odd):
        mine = lambda n, place: ((place[0] ^ (2 * n + odd)) * CORES + place[1], 0)
        return pl.BlockSpec((rows, span), mine), pl.BlockSpec((rows, 6 * PLANE), mine)

    def left_xy(odd, which, vecs, table, place):
        return pl.pallas_call(
            functools.partial(left_xy_kernel, momenta, rows, sites, which),
            grid_spec=pltpu.PrefetchScalarGridSpec(
                num_scalar_prefetch=1,
                grid=(half,),
                in_specs=[left_specs(odd)[0], whole(table), whole(phases)],
                out_specs=pl.BlockSpec((1, 4 * momenta * rows, span), lambda n, place: (n, 0, 0)),
                scratch_shapes=[pltpu.VMEM((18, PLANE), jnp.float32)],
            ),
            out_shape=left_shape,
            compiler_params=params,
            cost_estimate=cost(4e9 if odd == 0 else 0.5e9),
            name="left_xy",
        )(place, vecs, table, phases)

    def left_z(odd, sides):
        vec_spec, halo_spec = left_specs(odd)
        kept = pl.BlockSpec(memory_space=pl.ANY)
        return pl.pallas_call(
            functools.partial(left_z_kernel, momenta, rows, sites),
            grid_spec=pltpu.PrefetchScalarGridSpec(
                num_scalar_prefetch=1,
                grid=(half,),
                in_specs=[
                    vec_spec, vec_spec, halo_spec, halo_spec, whole(tables), whole(other_tables), whole(phases), kept, kept,
                ],
                out_specs=[pl.BlockSpec((1, 2 * momenta * rows, span), lambda n, place: (n, 2, 0))] * 2,
            ),
            out_shape=[left_shape] * 2,
            input_output_aliases={8: 0, 9: 1},
            compiler_params=params,
            cost_estimate=cost(5e9),
            name="left_z",
        )(place, flat, other, halo[0], halo[1], tables, other_tables, phases, *sides)

    def product(sides, mine, theirs, targets, kinds, first_row=0, size=left_rows, received=(), work=7e9):
        width = sum(piece.shape[0] for piece in mine)
        kept = pl.BlockSpec(memory_space=pl.ANY)
        in_vmem = pl.BlockSpec(memory_space=pltpu.VMEM)
        chunks = [sum(which == n for which, _ in targets) for n in range(len(kinds))]
        pairs = len(sides) // 2
        return pl.pallas_call(
            functools.partial(product_kernel, sites, half, first_row, size, len(mine), pairs, len(received), targets),
            in_specs=[kept] * (2 * len(mine) + len(sides)) + [in_vmem] * len(received),
            out_specs=[in_vmem] * len(kinds),
            out_shape=[jax.ShapeDtypeStruct((n, 2, size, width), kind) for n, kind in zip(chunks, kinds)],
            scratch_shapes=[
                pltpu.VMEM((2 * width, 2 * span), jnp.bfloat16),
                pltpu.VMEM((pairs * half * size, 2 * span), jnp.bfloat16),
                pltpu.SemaphoreType.DMA((2, len(mine))),
                pltpu.SemaphoreType.DMA((2, pairs * half)),
            ],
            compiler_params=params,
            cost_estimate=cost(work),
            name="product",
        )(*mine, *theirs, *sides, *received)

    def product_away(sides, right, first_row, size, work):
        (away,) = product(sides, *right, [(0, n) for n in range(half)], [jnp.bfloat16], first_row, size, work=work)
        return away, to_chip(away, 1)

    def product_home(sides, right, received, work):
        if half == 1:
            return product(sides, *right, [(0, 0)], [jnp.float32], received=received, work=work)
        targets = [(n % 2, n // 2) for n in range(half)]
        return product(sides, *right, targets, [jnp.float32, jnp.bfloat16], received=received, work=work)

    scale = 1.0 / math.sqrt(3.0 * sites * slabs)
    spots = 2 * (dirs % 3) + dirs // 3
    out_shape = jax.ShapeDtypeStruct((6, momenta, 2, rows, groups * count), jnp.float32)

    def finish(pieces, places, result):
        at = jnp.concatenate((spots, jnp.stack(places))).astype(jnp.int32)
        in_specs = [pl.BlockSpec((1, 2, left_rows, LANES), lambda n, at: (0, 0, 0, n))] * len(pieces)
        operands = list(pieces)
        aliases = {}
        if result is not None:
            in_specs.append(pl.BlockSpec(memory_space=pl.ANY))
            operands.append(result)
            aliases = {len(operands): 0}
        return pl.pallas_call(
            functools.partial(finish_kernel, len(pieces), momenta, rows, scale),
            grid_spec=pltpu.PrefetchScalarGridSpec(
                num_scalar_prefetch=1,
                grid=(len(places),),
                in_specs=in_specs,
                out_specs=pl.BlockSpec((6, momenta, 2, rows, LANES), lambda n, at: (0, 0, 0, 0, at[6 + n])),
            ),
            out_shape=out_shape,
            input_output_aliases=aliases,
            compiler_params=params,
            cost_estimate=cost(0.1e9),
            name="finish",
        )(at, *operands)

    def to_chip(array, bit):
        return lax.ppermute(array, "gz", [(i, i ^ (CORES * bit)) for i in range(slabs)])

    def from_group(array, turn):
        return lax.ppermute(array, "vec", [(i, i ^ turn) for i in range(groups)])

    def to_core(arrays):
        return [lax.ppermute(array, "gz", across) for array in arrays]

    def reduce_more(kept, away=None):
        if away is None:
            return [kept]
        pieces, bit = [(kept, 4), (to_chip(away, 2), 4)], 4
        while bit < chips:
            terms = [piece[bit // stride :: 2 * bit // stride].astype(jnp.float32) for piece, stride in pieces]
            away = functools.reduce(jnp.add, terms).astype(jnp.bfloat16)
            pieces.append((to_chip(away, bit), 2 * bit))
            bit *= 2
        return [piece for piece, _ in pieces]

    part = count // 2
    split = groups > 2 and part % LANES == 0
    if split:
        blocks = [[(1, 0), (2, 0)], [(1, 1), (2, 1)], [(3, 0), (3, 1)]] + [[(turn, None)] for turn in range(4, groups)]
    else:
        blocks = [[(turn, None)] for turn in range(1, groups)]
    source = {None: flat, 0: flat[:part], 1: flat[part:]}
    wide = count // LANES

    def columns(block):
        places = []
        for turn, which in block:
            at = (group ^ turn) * wide
            places += [at + n for n in range(wide)] if which is None else [at + which * (wide // 2) + n for n in range(wide // 2)]
        return places

    def fetch(block, *earlier):
        taken = []
        for turn, which in block:
            if split and turn == 3:
                piece, turn = (arriving[1][0], 2) if which == 0 else (arriving[2][1], 1)
            else:
                piece = source[which]
            taken.append(from_group(after(piece, *earlier) if earlier else piece, turn))
        return taken

    def own_columns(n):
        return columns([(0, None)] if n == 0 else blocks[n - 1])

    def pass_on(n, *earlier):
        if n not in arriving:
            return
        mine = [after(array, *earlier) for array in arriving[n]]
        if n < len(blocks):
            arriving[n + 1] = fetch(blocks[n], *mine)
        mine = [jnp.concatenate(mine, axis=0)] if len(mine) > 1 else mine
        right[n] = (mine, to_core(mine))

    last = len(blocks)
    arriving = {1: fetch(blocks[0])} if blocks else {}
    right = {0: ([flat], [other])}
    flat_rows = 4 * momenta * rows
    sides = {1: [None, None], 0: [None, None]}
    received, sums = {0: []}, {}
    done, held, result = place, (), None

    def run(step, n):
        nonlocal done, held, result
        now = (done, *held)
        if step not in ("pass", "halo"):
            held = ()
        if step == "left":
            odd, which = n
            vecs, table = ((flat, tables), (other, other_tables))[which]
            sides[odd][which] = done = left_xy(odd, which, vecs, table, after(place, *now))
        elif step == "left_z":
            sides[n] = left_z(n, [sides[n][0], after(sides[n][1], *now)])
            done = sides[n][0]
        elif step == "pass":
            pass_on(n, *now)
        elif step == "halo":
            halo[1] = lax.ppermute(after(halo[0], *now), "gz", across)
        elif step == "wait":
            held = (received[0][n] if n < 2 else sums[0][-1],)
        elif step == "finish":
            result = done = finish([after(sums[n][0], *now)] + sums[n][1:], own_columns(n), result)
        else:
            even = [after(sides[0][0], *now), sides[0][1]]
            odd = [after(sides[1][0], *now), sides[1][1]]
            if step == "xy":
                done, arrived = product_away(odd, right[n], 0, flat_rows, 1e9)
                received[n].append(arrived)
            elif step == "z":
                done, arrived = product_away(odd, right[n], flat_rows, left_rows - flat_rows, 2.5e9)
                received[n].append(arrived)
            elif step == "away":
                done, arrived = product_away(odd, right[n], 0, left_rows, 3e9)
                received[n] = [arrived]
            elif step == "home":
                outs = product_home(even, right[n], received[n], 4e9)
                sums[n], done = reduce_more(*outs), outs[0]

    for step, n in order(last):
        run(step, n)
    return result


def solution(mesh):
    placed = (P("vec", None, None, "gz"), P(None, None, None, None, "gz"), P(), P())
    return jax.shard_map(
        on_device,
        mesh=mesh,
        in_specs=placed,
        out_specs=P(None, None, None, ("vec", "gz"), None),
        check_vma=False,
    )
```
